32 devices in a mesh: dp: 8 (over y, x, core), sp: 4 (over z).
Axes of the slice: x: 2, y: 2, z: 4, core: 2. Of those that a mesh axis runs over, the one named last changes fastest.
Arguments:
- inputs: bfloat16 [8, 1024, 2048], P('dp', 'sp'), may hold values from -6 to 6
- cotangent: bfloat16 [8, 1024, 2048], P('dp', 'sp'), may hold values from -6 to 6
- unit_lengths: int32 [8, 2], P('dp'), may hold values from 1 to 6, 8 in all within a row
- attn_gain: bfloat16 [2048], P(('dp', 'sp')), may hold values from 0.25 to 1.75
- w_query: bfloat16 [2048, 2048], P(('dp', 'sp')), may hold values from -0.125 to 0.125
- key_weight: bfloat16 [2048, 256], P(('dp', 'sp')), may hold values from -0.125 to 0.125
- value_weight: bfloat16 [2048, 256], P(('dp', 'sp')), may hold values from -0.125 to 0.125
- w_output: bfloat16 [2048, 2048], P(('dp', 'sp')), may hold values from -0.75 to 0.75
- mlp_gain: bfloat16 [2048], P(('dp', 'sp')), may hold values from 0.25 to 1.75
- w_gate: bfloat16 [2048, 5632], P(('dp', 'sp')), may hold values from -0.125 to 0.125
- w_up: bfloat16 [2048, 5632], P(('dp', 'sp')), may hold values from -0.125 to 0.125
- w_down: bfloat16 [2048, 5632], P(('dp', 'sp')), may hold values from -0.078125 to 0.078125
Outputs:
- output: bfloat16 [8, 1024, 2048], P('dp', 'sp')
- input_grad: bfloat16 [8, 1024, 2048], P('dp', 'sp')
- grad_attn_gain: float32 [2048], P(('dp', 'sp'))
- grad_query: float32 [2048, 2048], P(('dp', 'sp'))
- grad_key: float32 [2048, 256], P(('dp', 'sp'))
- grad_value: float32 [2048, 256], P(('dp', 'sp'))
- grad_output_proj: float32 [2048, 2048], P(('dp', 'sp'))
- grad_mlp_gain: float32 [2048], P(('dp', 'sp'))
- grad_gate: float32 [2048, 5632], P(('dp', 'sp'))
- grad_up: float32 [2048, 5632], P(('dp', 'sp'))
- grad_down: float32 [2048, 5632], P(('dp', 'sp'))
The draws below stay inside these ranges and needn't reach their ends.
Inputs may be any that keep to these rules, and one draw needn't show every extreme that they name: `unit_lengths`: each row's 2 lengths, in units of 128 tokens, sum to 8; the longest in every row is at most 6.
All inputs are finite; a program needn't handle non-finite values.
Results may differ from the reference program's by a relative error of at most 0.015.
Values may be sent and summed in bfloat16 or wider, within the bound.
No kernel may reach another device: no remote copies, remote signals or barrier semaphores. Data moves between devices by JAX's collectives and lax.ppermute only.
A program may use at most 576 MiB of HBM per device.

```python
import math
import jax
import jax.numpy as jnp
import numpy as np
from jax import lax

MODEL_WIDTH = 2048
HQ = 32
KEY_VALUE_HEADS = 4
HEAD_SIZE = 64
FF = 5632
UNIT = 128
QBLOCK = 512
ROWS = 8
LENGTH = 1024
ROW_UNITS = 8
LONGEST = 6
DOCS = 2
HEAD_COPIES = 4


def levels(stream_key, extent, pieces, least, largest):
    gain = 1.0
    for dim, blocks in pieces:
        heights = jax.random.uniform(jax.random.fold_in(jax.random.fold_in(stream_key, 6), dim), (blocks,), jnp.float32, least / len(pieces), largest / len(pieces))
        gain = gain * jnp.repeat(jnp.exp(heights), extent[dim] // blocks).reshape((-1,) + (1,) * (len(extent) - 1 - dim))
    return gain


def split_up(count, total, most, skew):
    weights = [(1 << 20) // math.isqrt(rank ** skew) + 1 for rank in range(2, count + 1)]
    surplus, holding = total - most - (count - 1), [1] * (count - 1)
    while surplus > 0:
        movable = [i for i in range(count - 1) if holding[i] < most]
        pool, left = sum([weights[i] for i in movable]), surplus
        for i in movable:
            more = min(most - holding[i], max(1, left * weights[i] // pool), surplus)
            holding[i] = holding[i] + more
            surplus = surplus - more
    return np.array([most] + holding)


def uneven_parts(rng, amount, total, bound, slope):
    if amount == 2:
        one = jax.random.randint(rng, (), max(1, total - bound), min(bound, total - 1) + 1)
        return jnp.stack([one, total - one])
    sizes = jnp.asarray(split_up(amount, total, bound, slope), jnp.int32)
    pairs = (amount - 1) // 2
    donor, sink = sizes[1:1 + 2 * pairs:2], sizes[2:2 + 2 * pairs:2]
    margin = jnp.minimum(donor - 1, bound - sink)
    moved = jax.random.randint(jax.random.fold_in(rng, 1), (pairs,), 0, 1 << 20) % (margin + 1)
    sizes = sizes.at[1:1 + 2 * pairs:2].set(donor - moved).at[2:2 + 2 * pairs:2].set(sink + moved)
    return sizes[jax.random.permutation(jax.random.fold_in(rng, 2), amount)]


def noise(rng, shape, spread, limit, shards=(), kind=jnp.bfloat16):
    factor_of = levels(rng, shape, shards, -0.22, 0.18) if shards else 1.0
    values = jax.random.normal(rng, shape, jnp.float32) * spread * factor_of
    return jnp.minimum(jnp.maximum(values, -limit), limit).astype(kind)


def setup_inputs(seed: int = 0) -> dict:
    splits = jax.random.split(jax.random.key(seed), 13)
    return {
        "inputs": noise(splits[0], (ROWS, LENGTH, MODEL_WIDTH), 1.0, 6.0, ((0, 8), (1, 4))),
        "cotangent": noise(splits[1], (ROWS, LENGTH, MODEL_WIDTH), 1.0, 6.0, ((0, 8), (1, 4))),
        "unit_lengths": jax.vmap(lambda own: uneven_parts(own, DOCS, ROW_UNITS, LONGEST, 2))(jax.random.split(splits[2], ROWS)).reshape((ROWS, DOCS)).astype(jnp.int32),
        "attn_gain": jnp.clip(1.0 + 0.15 * jax.random.normal(splits[3], (MODEL_WIDTH,), jnp.float32), 0.25, 1.75).astype(jnp.bfloat16),
        "w_query": noise(splits[4], (MODEL_WIDTH, HQ * HEAD_SIZE), MODEL_WIDTH ** -0.5, 0.125, ((0, 32),)),
        "key_weight": noise(splits[5], (MODEL_WIDTH, KEY_VALUE_HEADS * HEAD_SIZE), MODEL_WIDTH ** -0.5, 0.125, ((0, 32),)),
        "value_weight": noise(splits[6], (MODEL_WIDTH, KEY_VALUE_HEADS * HEAD_SIZE), MODEL_WIDTH ** -0.5, 0.125, ((0, 32),)),
        "w_output": noise(splits[7], (MODEL_WIDTH, HQ * HEAD_SIZE), (max(16, MODEL_WIDTH // 32)) ** -0.5, 0.75, ((0, 32),)),
        "mlp_gain": jnp.clip(1.0 + 0.15 * jax.random.normal(splits[8], (MODEL_WIDTH,), jnp.float32), 0.25, 1.75).astype(jnp.bfloat16),
        "w_gate": noise(splits[9], (MODEL_WIDTH, FF), MODEL_WIDTH ** -0.5, 0.125, ((0, 32),)),
        "w_up": noise(splits[10], (MODEL_WIDTH, FF), MODEL_WIDTH ** -0.5, 0.125, ((0, 32),)),
        "w_down": noise(splits[11], (MODEL_WIDTH, FF), FF ** -0.5, 0.078125, ((0, 32),)),
    }


EPSILON = 1e-05
MASKED = -1e+30
HIGHEST = lax.Precision.HIGHEST

@jax.custom_vjp
def lower_precision(v):
    return lax.optimization_barrier(v.astype(jnp.bfloat16)).astype(jnp.float32)

@jax.custom_vjp
def lower_precision_backward(v):
    return v

def low_keep(v):
    return (lower_precision(v), None)

def low_pass(kept, grad):
    return (grad,)

def back_keep(v):
    return (v, None)

def back_low(kept, grad):
    return (lower_precision(grad),)
lower_precision.defvjp(low_keep, low_pass)
lower_precision_backward.defvjp(back_keep, back_low)

def doc_layout(unit_lengths, document_length):
    token_lengths = (unit_lengths * UNIT).astype(jnp.int32)
    ends = jnp.cumsum(token_lengths).astype(jnp.int32)
    places = jnp.arange(document_length, dtype=jnp.int32)
    passed = places[:, None] >= ends[None, :]
    segment = lax.optimization_barrier(jnp.sum(passed.astype(jnp.int32), axis=1)).astype(jnp.int32)
    begins = lax.optimization_barrier(jnp.sum(jnp.where(passed, token_lengths[None, :], 0), axis=1)).astype(jnp.int32)
    return (segment, places - begins)

def rope_tables(positions):
    half_dim = HEAD_SIZE // 2
    inverse = jnp.power(10000.0, jnp.arange(half_dim, dtype=jnp.float32) * (-2.0 / HEAD_SIZE))
    angles = positions.astype(jnp.float32)[:, None] * inverse[None, :]
    cos_half = jnp.cos(angles)
    sin_half = jnp.sin(angles)
    return (jnp.concatenate([cos_half, cos_half], 1), jnp.concatenate([sin_half, sin_half], 1))

def apply_rotary(values, cosine_table, sine_table):
    half_dim = HEAD_SIZE // 2
    turned = jnp.concatenate([-values[..., half_dim:], values[..., :half_dim]], -1)
    return values * cosine_table[:, None, :] + turned * sine_table[:, None, :]

def attention(query, key_slots, value_copies, segment):
    document_length = query.shape[0]
    grouped = query.reshape(document_length, HEAD_COPIES, HQ // HEAD_COPIES, HEAD_SIZE)
    places = jnp.arange(document_length, dtype=jnp.int32)

    def one_block(block):
        q_start = block * QBLOCK
        query_block = lax.dynamic_slice_in_dim(grouped, q_start, QBLOCK, 0)
        scores = jnp.einsum('qsgd,ksd->sgqk', query_block, key_slots, precision=HIGHEST) * HEAD_SIZE ** (-0.5)
        scores = lower_precision_backward(scores)
        seg_query = lax.dynamic_slice_in_dim(segment, q_start, QBLOCK, 0)
        at_query = lax.dynamic_slice_in_dim(places, q_start, QBLOCK, 0)
        allowed = (seg_query[:, None] == segment[None, :]) & (places[None, :] <= at_query[:, None])
        scores = jnp.where(allowed[None, None], scores, MASKED)
        probabilities = lower_precision(jax.nn.softmax(scores, axis=-1))
        return jnp.einsum('sgqk,ksd->qsgd', probabilities, value_copies, precision=HIGHEST)
    blocks = lax.map(jax.checkpoint(one_block), jnp.arange(document_length // QBLOCK, dtype=jnp.int32))
    return blocks.reshape(document_length, HQ * HEAD_SIZE)

def layer(tokens_in, segment, positions, attn_gain, w_query, key_weight, value_weight, w_output, mlp_gain, w_gate, w_up, w_down):
    document_length = tokens_in.shape[0]
    head_copies = HEAD_COPIES // KEY_VALUE_HEADS
    inv_one = lax.rsqrt(lax.optimization_barrier(jnp.mean(tokens_in * tokens_in, axis=1, keepdims=True)) + EPSILON)
    normed_one = lower_precision(tokens_in * inv_one * attn_gain)
    query_pre = lower_precision_backward(jnp.dot(normed_one, w_query, precision=HIGHEST))
    key_before_rotary = lower_precision_backward(jnp.dot(normed_one, key_weight, precision=HIGHEST))
    value_before_copy = lower_precision_backward(jnp.dot(normed_one, value_weight, precision=HIGHEST))
    cosine_table, sine_table = rope_tables(positions)
    query = lower_precision(lower_precision_backward(apply_rotary(query_pre.reshape(document_length, HQ, HEAD_SIZE), cosine_table, sine_table)))
    key_rotated = apply_rotary(key_before_rotary.reshape(document_length, KEY_VALUE_HEADS, HEAD_SIZE), cosine_table, sine_table)
    key_slots = lower_precision(lower_precision_backward(jnp.repeat(key_rotated, head_copies, axis=1)))
    value_copies = lower_precision(lower_precision_backward(jnp.repeat(value_before_copy.reshape(document_length, KEY_VALUE_HEADS, HEAD_SIZE), head_copies, axis=1)))
    attended = lower_precision(lower_precision_backward(attention(query, key_slots, value_copies, segment)))
    attn_out = jnp.dot(attended, w_output.T, precision=HIGHEST)
    resid = tokens_in + lower_precision_backward(attn_out)
    inv_two = lax.rsqrt(lax.optimization_barrier(jnp.mean(resid * resid, axis=1, keepdims=True)) + EPSILON)
    normed_two = lower_precision(resid * inv_two * mlp_gain)
    gate_value = lower_precision_backward(jnp.dot(normed_two, w_gate, precision=HIGHEST))
    up_value = lower_precision_backward(jnp.dot(normed_two, w_up, precision=HIGHEST))
    hidden = lower_precision(jax.nn.silu(gate_value) * up_value)
    mlp_out = jnp.dot(hidden, w_down.T, precision=HIGHEST)
    return resid + lower_precision_backward(mlp_out)

def reference(inputs, cotangent, unit_lengths, attn_gain, w_query, key_weight, value_weight, w_output, mlp_gain, w_gate, w_up, w_down):
    weights = tuple((weight.astype(jnp.float32) for weight in (attn_gain, w_query, key_weight, value_weight, w_output, mlp_gain, w_gate, w_up, w_down)))

    def one_row(totals, row_data):
        tokens_row, grad_row, lengths_row = row_data
        segment, positions = doc_layout(lengths_row, tokens_row.shape[0])

        def forward(tokens_float, *params):
            return layer(tokens_float, segment, positions, *params)
        result, pullback = jax.vjp(forward, tokens_row.astype(jnp.float32), *weights)
        grads = pullback(grad_row.astype(jnp.float32))
        totals = tuple((total + grad for total, grad in zip(totals, grads[1:])))
        return (totals, (result.astype(jnp.bfloat16), grads[0].astype(jnp.bfloat16)))
    zeros = tuple((jnp.zeros(weight.shape, jnp.float32) for weight in weights))
    totals, (outputs, input_grads) = lax.scan(one_row, zeros, (inputs, cotangent, unit_lengths))
    return (outputs, input_grads, totals[0], totals[1], totals[2], totals[3], totals[4], totals[5], totals[6], totals[7], totals[8])
```

```python
import jax
import jax.numpy as jnp
from jax import lax
from jax.sharding import PartitionSpec as P

HQ = 32
KEY_VALUE_HEADS = 4
HEAD_SIZE = 64
UNIT = 128

EPSILON = 1e-05
MASKED = -1e30
F32 = jnp.float32
BF16 = jnp.bfloat16
BOTH = ("dp", "sp")


def doc_layout(unit_lengths, places):
    token_lengths = unit_lengths * UNIT
    ends = jnp.cumsum(token_lengths)
    passed = places[:, None] >= ends[None, :]
    segment = jnp.sum(passed.astype(jnp.int32), axis=1)
    begins = jnp.sum(jnp.where(passed, token_lengths[None, :], 0), axis=1)
    return segment, places - begins


def rope_tables(positions):
    half_dim = HEAD_SIZE // 2
    inverse = jnp.power(10000.0, jnp.arange(half_dim, dtype=F32) * (-2.0 / HEAD_SIZE))
    angles = positions.astype(F32)[:, None] * inverse[None, :]
    cos_half = jnp.cos(angles)
    sin_half = jnp.sin(angles)
    return jnp.concatenate([cos_half, cos_half], 1), jnp.concatenate([sin_half, sin_half], 1)


def apply_rotary(values, cosine_table, sine_table):
    half_dim = HEAD_SIZE // 2
    turned = jnp.concatenate([-values[..., half_dim:], values[..., :half_dim]], -1)
    return values * cosine_table[:, None, :] + turned * sine_table[:, None, :]


def unrotate(grads, cosine_table, sine_table):
    half_dim = HEAD_SIZE // 2
    scaled = grads * sine_table[:, None, :]
    turned = jnp.concatenate([scaled[..., half_dim:], -scaled[..., :half_dim]], -1)
    return grads * cosine_table[:, None, :] + turned


def contract_last(left, right):
    return lax.dot_general(left, right, (((1,), (1,)), ((), ())), preferred_element_type=F32)


def contract_rows(left, right):
    return lax.dot_general(left, right, (((0,), (0,)), ((), ())), preferred_element_type=F32)


def flip(value, count, bit):
    return lax.ppermute(value, "dp", [(i, i ^ bit) for i in range(count)])


def bit_orders(count):
    high = [1 << b for b in range(1, count.bit_length() - 1)]
    return high + [1], high[::-1] + [1]


def plane_gather(value, count):
    half = value.shape[0] // 2
    orders = bit_orders(count)
    held = [{0: value[:half]}, {0: value[half:]}]
    for step in range(len(orders[0])):
        for part in (0, 1):
            bit = orders[part][step]
            held[part].update({k ^ bit: flip(v, count, bit) for k, v in list(held[part].items())})
    return jnp.concatenate([held[part][k] for part in (0, 1) for k in range(count)], axis=0)


def plane_scatter(partial, count):
    half = partial.shape[0] // (2 * count)
    orders = bit_orders(count)
    held = [
        {k: partial[(part * count + k) * half : (part * count + k + 1) * half] for k in range(count)}
        for part in (0, 1)
    ]
    for step in reversed(range(len(orders[0]))):
        for part in (0, 1):
            bit = orders[part][step]
            group = held[part]
            sent = {k ^ bit: flip(group.pop(k).astype(BF16), count, bit) for k in list(group) if k & bit}
            for k, v in sent.items():
                group[k] = group[k].astype(F32) + v.astype(F32)
    return jnp.concatenate([held[0][0], held[1][0]], axis=0)


def shift(value, count, by):
    pairs = [(i, i + by) for i in range(count) if 0 <= i + by < count]
    return lax.ppermute(value, "sp", pairs)


def local(
    inputs,
    cotangent,
    unit_lengths,
    attn_gain,
    w_query,
    key_weight,
    value_weight,
    w_output,
    mlp_gain,
    w_gate,
    w_up,
    w_down,
):
    dp_count = lax.axis_size("dp")
    sp_count = lax.axis_size("sp")
    sp_index = lax.axis_index("sp")
    shard = inputs.shape[1]
    width = inputs.shape[2]
    length = shard * sp_count
    rows = w_query.shape[0]
    ff = w_gate.shape[1]
    ff_local = ff // dp_count
    query_width = HQ * HEAD_SIZE
    key_width = KEY_VALUE_HEADS * HEAD_SIZE
    project_width = query_width + 2 * key_width
    group = HQ // KEY_VALUE_HEADS
    scale = HEAD_SIZE ** (-0.5)

    gains_local = jnp.stack([attn_gain, mlp_gain], axis=1)
    in_local = jnp.concatenate(
        [w_query, key_weight, value_weight, jnp.pad(gains_local, ((0, 0), (0, 126)))], axis=1
    )
    in_all = lax.all_gather(in_local, BOTH, axis=0, tiled=True)
    out_weight = lax.all_gather(w_output, BOTH, axis=0, tiled=True)
    in_weight = in_all[:, :project_width]
    gains = in_all[:, project_width : project_width + 2].astype(F32).T
    gain_one, gain_two = gains[0][None], gains[1][None]

    def by_columns(weights):
        split = jnp.concatenate([w.reshape(rows, dp_count, ff_local) for w in weights], axis=2)
        exchanged = lax.all_to_all(split, "dp", split_axis=1, concat_axis=0, tiled=True)
        exchanged = exchanged.reshape(dp_count, rows, split.shape[2])
        gathered = lax.all_gather(exchanged, "sp", axis=0)
        return gathered.transpose(1, 0, 2, 3).reshape(width, split.shape[2])

    both_weight = by_columns([w_gate, w_up])
    down_weight = by_columns([w_down])
    gate_weight, up_weight = both_weight[:, :ff_local], both_weight[:, ff_local:]

    places = sp_index * shard + jnp.arange(shard, dtype=jnp.int32)
    segment, positions = doc_layout(unit_lengths[0], places)
    cosine_table, sine_table = rope_tables(positions)
    tokens_in = inputs[0].astype(F32)
    inv_one = lax.rsqrt(jnp.mean(tokens_in * tokens_in, axis=1, keepdims=True) + EPSILON)
    normed_one = (tokens_in * inv_one * gain_one).astype(BF16)
    project = jnp.dot(normed_one, in_weight, preferred_element_type=F32)
    query = apply_rotary(
        project[:, :query_width].reshape(shard, HQ, HEAD_SIZE), cosine_table, sine_table
    ).astype(BF16)
    key = apply_rotary(
        project[:, query_width : query_width + key_width].reshape(shard, KEY_VALUE_HEADS, HEAD_SIZE),
        cosine_table,
        sine_table,
    )
    key_value = jnp.concatenate(
        [key.reshape(shard, key_width), project[:, query_width + key_width :]], axis=1
    ).astype(BF16)
    key_values = jnp.concatenate(
        [key_value] + [shift(key_value, sp_count, j) for j in range(1, sp_count)], axis=0
    )
    keys = key_values[:, :key_width].reshape(length, KEY_VALUE_HEADS, HEAD_SIZE)
    values = key_values[:, key_width:].reshape(length, KEY_VALUE_HEADS, HEAD_SIZE)
    key_places = jnp.concatenate([places - j * shard for j in range(sp_count)])
    key_segment, _ = doc_layout(unit_lengths[0], key_places)
    allowed = (
        (segment[:, None] == key_segment[None, :])
        & (key_places[None, :] <= places[:, None])
        & (key_places[None, :] >= 0)
    )
    queries = query.reshape(shard, KEY_VALUE_HEADS, group, HEAD_SIZE)
    scores = jnp.einsum("qsgd,ksd->sgqk", queries, keys, preferred_element_type=F32) * scale
    scores = jnp.where(allowed[None, None], scores, MASKED)
    largest = jnp.max(scores, axis=3, keepdims=True)
    exped = jnp.exp(scores - largest)
    totals = jnp.sum(exped, axis=3, keepdims=True)
    probs = (exped / totals).astype(BF16)
    log_totals = largest + jnp.log(totals)
    attended = jnp.einsum("sgqk,ksd->qsgd", probs, values, preferred_element_type=F32)
    attended = attended.astype(BF16).reshape(shard, query_width)
    resid = tokens_in + contract_last(attended, out_weight)

    inv_two = lax.rsqrt(jnp.mean(resid * resid, axis=1, keepdims=True) + EPSILON)
    normed_two = (resid * inv_two * gain_two).astype(BF16)
    grad_out = cotangent[0]
    plane_grad = plane_gather(grad_out, dp_count)
    plane_normed = plane_gather(normed_two, dp_count)
    gate = jnp.dot(plane_normed, gate_weight, preferred_element_type=F32)
    up = jnp.dot(plane_normed, up_weight, preferred_element_type=F32)
    d_hidden = jnp.dot(plane_grad, down_weight, preferred_element_type=F32)
    sigmoid_gate = jax.nn.sigmoid(gate)
    activated = gate * sigmoid_gate
    hidden = (activated * up).astype(BF16)
    d_gate = (d_hidden * up * (sigmoid_gate * (1.0 + gate * (1.0 - sigmoid_gate)))).astype(BF16)
    d_up = (d_hidden * activated).astype(BF16)
    d_normed_part = contract_last(d_gate, gate_weight) + contract_last(d_up, up_weight)
    d_normed_two = plane_scatter(d_normed_part.astype(BF16), dp_count)
    mlp_out = plane_scatter(contract_last(hidden, down_weight).astype(BF16), dp_count)
    output = (resid + mlp_out).astype(BF16)

    mixed_two = d_normed_two * gain_two
    d_resid = (
        grad_out.astype(F32)
        + inv_two * mixed_two
        - resid * (inv_two * inv_two * inv_two) * jnp.mean(mixed_two * resid, axis=1, keepdims=True)
    )
    d_attn_out = d_resid.astype(BF16)

    d_attended = jnp.dot(d_attn_out, out_weight, preferred_element_type=F32).astype(BF16)
    d_heads = d_attended.reshape(shard, KEY_VALUE_HEADS, group, HEAD_SIZE)
    scores = jnp.einsum("qsgd,ksd->sgqk", queries, keys, preferred_element_type=F32) * scale
    scores = jnp.where(allowed[None, None], scores, MASKED)
    probabilities = jnp.exp(scores - log_totals)
    d_probs = jnp.einsum("qsgd,ksd->sgqk", d_heads, values, preferred_element_type=F32)
    row_dot = jnp.sum(probabilities * d_probs, axis=3, keepdims=True)
    d_scores = (probabilities * (d_probs - row_dot)).astype(BF16)
    d_query = jnp.einsum("sgqk,ksd->qsgd", d_scores, keys, preferred_element_type=F32) * scale
    d_keys = jnp.einsum("sgqk,qsgd->ksd", d_scores, queries, preferred_element_type=F32) * scale
    d_values = jnp.einsum(
        "sgqk,qsgd->ksd", probabilities.astype(BF16), d_heads, preferred_element_type=F32
    )
    d_key_values = jnp.concatenate(
        [d_keys.reshape(length, key_width), d_values.reshape(length, key_width)], axis=1
    )
    d_key_value = d_key_values[:shard]
    for j in range(1, sp_count):
        sent = d_key_values[j * shard : (j + 1) * shard].astype(BF16)
        d_key_value = d_key_value + shift(sent, sp_count, -j).astype(F32)
    d_query_pre = unrotate(
        d_query.reshape(shard, HQ, HEAD_SIZE).astype(BF16).astype(F32), cosine_table, sine_table
    )
    d_key_pre = unrotate(
        d_key_value[:, :key_width].reshape(shard, KEY_VALUE_HEADS, HEAD_SIZE),
        cosine_table,
        sine_table,
    )
    d_project = jnp.concatenate(
        [
            d_query_pre.reshape(shard, query_width),
            d_key_pre.reshape(shard, key_width),
            d_key_value[:, key_width:],
        ],
        axis=1,
    ).astype(BF16)
    d_normed_one = contract_last(d_project, in_weight)
    mixed_one = d_normed_one * gain_one
    input_grad = (
        d_resid
        + inv_one * mixed_one
        - tokens_in
        * (inv_one * inv_one * inv_one)
        * jnp.mean(mixed_one * tokens_in, axis=1, keepdims=True)
    ).astype(BF16)

    def column_grads(left, rights):
        total = jnp.concatenate([contract_rows(left, r).astype(BF16) for r in rights], axis=1)
        columns = total.shape[1]
        total = total.reshape(dp_count, sp_count, rows, columns).transpose(1, 0, 2, 3)
        summed = lax.psum_scatter(
            total.reshape(width, columns), "sp", scatter_dimension=0, tiled=True
        ).reshape(dp_count, rows, columns)
        back = lax.all_to_all(summed, "dp", split_axis=0, concat_axis=0, tiled=True)
        back = back.transpose(1, 0, 2).astype(F32)
        results, start = [], 0
        for r in rights:
            results.append(back[:, :, start : start + r.shape[1]].reshape(rows, -1))
            start += r.shape[1]
        return results

    (grad_down,) = column_grads(plane_grad, [hidden])
    grad_gate, grad_up = column_grads(plane_normed, [d_gate, d_up])
    attended_plane = lax.all_gather(attended, "dp", axis=0, tiled=True)
    normed_plane = lax.all_gather(normed_one, "dp", axis=0, tiled=True)
    out_rows = lax.all_to_all(
        d_attn_out.reshape(shard, dp_count, width // dp_count), "dp", split_axis=1, concat_axis=0, tiled=True
    ).reshape(shard * dp_count, width // dp_count)
    grad_output_proj = lax.psum_scatter(
        contract_rows(out_rows, attended_plane).astype(BF16), "sp", scatter_dimension=0, tiled=True
    ).astype(F32)
    project_columns = lax.all_to_all(
        d_project.reshape(shard, dp_count, project_width // dp_count),
        "dp",
        split_axis=1,
        concat_axis=0,
        tiled=True,
    ).reshape(shard * dp_count, project_width // dp_count)
    (grad_project,) = column_grads(normed_plane, [project_columns])
    grad_query = grad_project[:, :query_width]
    grad_key = grad_project[:, query_width : query_width + key_width]
    grad_value = grad_project[:, query_width + key_width :]
    grad_attn_gain = (
        jnp.sum(w_query.astype(F32) * grad_query, axis=1)
        + jnp.sum(key_weight.astype(F32) * grad_key, axis=1)
        + jnp.sum(value_weight.astype(F32) * grad_value, axis=1)
    ) / attn_gain.astype(F32)
    grad_mlp_gain = (
        jnp.sum(w_gate.astype(F32) * grad_gate, axis=1) + jnp.sum(w_up.astype(F32) * grad_up, axis=1)
    ) / mlp_gain.astype(F32)
    return (
        output[None],
        input_grad[None],
        grad_attn_gain,
        grad_query,
        grad_key,
        grad_value,
        grad_output_proj,
        grad_mlp_gain,
        grad_gate,
        grad_up,
        grad_down,
    )


def solution(mesh):
    token_spec = P("dp", "sp", None)
    vector_spec = P(BOTH)
    weight_spec = P(BOTH, None)
    return jax.shard_map(
        local,
        mesh=mesh,
        in_specs=(
            token_spec,
            token_spec,
            P("dp", None),
            vector_spec,
            weight_spec,
            weight_spec,
            weight_spec,
            weight_spec,
            vector_spec,
            weight_spec,
            weight_spec,
            weight_spec,
        ),
        out_specs=(
            token_spec,
            token_spec,
            vector_spec,
            weight_spec,
            weight_spec,
            weight_spec,
            weight_spec,
            vector_spec,
            weight_spec,
            weight_spec,
            weight_spec,
        ),
        check_vma=False,
    )
```

```python
import jax
import jax.numpy as jnp
from jax import lax
from jax.experimental import pallas as pl
from jax.experimental.pallas import tpu as pltpu
from jax.sharding import Mesh, PartitionSpec as P

HQ = 32
KEY_VALUE_HEADS = 4
HEAD_SIZE = 64
UNIT = 128
DOC_UNITS = 8
LANES = 128
GROUP = HQ // KEY_VALUE_HEADS
QUERY_WIDTH = HQ * HEAD_SIZE
KEY_WIDTH = KEY_VALUE_HEADS * HEAD_SIZE
PROJECT = QUERY_WIDTH + 2 * KEY_WIDTH
BLOCK = GROUP * HEAD_SIZE

EPSILON = 1e-05
MASKED = -1e30
SCALE = HEAD_SIZE ** (-0.5)
F32 = jnp.float32
BF16 = jnp.bfloat16
MEMBERS = ("chip", "core")
EVERY = ("chip", "core", "sp")
VMEM_LIMIT = 48 * 1024 * 1024
NO_COST = pl.CostEstimate(flops=0, bytes_accessed=0, transcendentals=0)


def cost(flops):
    return pl.CostEstimate(flops=int(flops), bytes_accessed=0, transcendentals=0)


def doc_layout(unit_lengths, places):
    token_lengths = unit_lengths * UNIT
    ends = jnp.cumsum(token_lengths)
    passed = places[:, None] >= ends[None, :]
    return jnp.sum(jnp.where(passed, token_lengths[None, :], 0), axis=1)


def rope_tables(positions):
    half_dim = HEAD_SIZE // 2
    inverse = jnp.power(10000.0, jnp.arange(half_dim, dtype=F32) * (-2.0 / HEAD_SIZE))
    angles = positions.astype(F32)[:, None] * inverse[None, :]
    return jnp.tile(jnp.cos(angles), (1, 4)), jnp.tile(jnp.sin(angles), (1, 4))


def key_pieces(length, shard, docs):
    units, per = length // UNIT, shard // UNIT
    longest = min(DOC_UNITS, units - 2)
    needed = 1
    for unit in range(units):
        earliest = max(0, unit - longest + 1)
        if docs == 2 and unit >= longest:
            earliest = max(earliest, units - longest)
        needed = max(needed, unit // per - earliest // per + 1)
    return needed


def contract_last(left, right):
    return lax.dot_general(left, right, (((1,), (1,)), ((), ())), preferred_element_type=F32)


def contract_rows(left, right):
    return lax.dot_general(left, right, (((0,), (0,)), ((), ())), preferred_element_type=F32)


def first_half(shape):
    lane = lax.broadcasted_iota(jnp.int32, shape, 1)
    return lane % HEAD_SIZE < HEAD_SIZE // 2


def half_swap(values):
    half_dim, lanes = HEAD_SIZE // 2, values.shape[1]
    return jnp.where(
        first_half(values.shape),
        pltpu.roll(values, lanes - half_dim, 1),
        pltpu.roll(values, half_dim, 1),
    )


def member_product(by_rows, chips, values, own, other, core, extras, out_shapes, finish, name):
    tokens = values.shape[0]
    block, columns = own.shape[0] // chips, own.shape[1]
    width = columns if by_rows else 2 * own.shape[0]

    def kernel(core_ref, values_ref, own_ref, other_ref, *refs):
        extra_refs, out_refs, total_ref = refs[: len(extras)], refs[len(extras) : -1], refs[-1]
        chip, mine = pl.program_id(0), core_ref[0]
        places = [
            pl.ds(pl.multiple_of((chip * 2 + c) * block, LANES), block) for c in (mine, 1 - mine)
        ]
        if by_rows:
            part = jnp.dot(values_ref[:, places[0]], own_ref[...], preferred_element_type=F32)
            part = part + jnp.dot(values_ref[:, places[1]], other_ref[...], preferred_element_type=F32)

            @pl.when(chip == 0)
            def _():
                total_ref[...] = part

            @pl.when(chip > 0)
            def _():
                total_ref[...] += part
        else:
            used = values_ref.shape[1]
            total_ref[:, places[0]] = contract_last(values_ref[...], own_ref[:, :used])
            total_ref[:, places[1]] = contract_last(values_ref[...], other_ref[:, :used])

        @pl.when(chip == chips - 1)
        def _():
            finish(total_ref, extra_refs, out_refs)

    def whole(shape):
        return pl.BlockSpec(shape, lambda i: (0,) * len(shape))

    return pl.pallas_call(
        kernel,
        grid=(chips,),
        in_specs=[
            pl.BlockSpec(memory_space=pltpu.SMEM),
            whole(values.shape),
            pl.BlockSpec((block, columns), lambda i: (i, 0)),
            pl.BlockSpec((block, columns), lambda i: (i, 0)),
        ]
        + [whole(e.shape) for e in extras],
        out_specs=[whole(o.shape) for o in out_shapes],
        out_shape=out_shapes,
        scratch_shapes=[pltpu.VMEM((tokens, width), F32)],
        compiler_params=pltpu.CompilerParams(vmem_limit_bytes=VMEM_LIMIT),
        cost_estimate=NO_COST,
        name=name,
    )(core, values, own, other, *extras)


def project_kernel(
    core_ref, scaled_ref, own_ref, other_ref, cos_ref, sin_ref, out_ref, normed_ref, gains_ref, total_ref
):
    chip, mine = pl.program_id(0), core_ref[0]
    block = own_ref.shape[0]
    part = None
    for ref, c in ((own_ref, mine), (other_ref, 1 - mine)):
        place = pl.ds(pl.multiple_of((chip * 2 + c) * block, LANES), block)
        gains = ref[:, PROJECT : PROJECT + LANES].astype(F32).T[:8]
        gains_ref[:, place] = gains
        normed = (scaled_ref[:, place] * gains[:1]).astype(BF16)
        normed_ref[:, place] = normed
        term = jnp.dot(normed, ref[:, :PROJECT], preferred_element_type=F32)
        part = term if part is None else part + term

    @pl.when(chip == 0)
    def _():
        total_ref[...] = part

    @pl.when(chip > 0)
    def _():
        total_ref[...] += part

    @pl.when(chip == pl.num_programs(0) - 1)
    def _():
        cosine = jnp.concatenate([cos_ref[...]] * (BLOCK // LANES), axis=1)
        sine = jnp.concatenate([sin_ref[...]] * (BLOCK // LANES), axis=1)
        for step in range(PROJECT // BLOCK):
            where = slice(step * BLOCK, (step + 1) * BLOCK)
            values = total_ref[:, where]
            swapped = half_swap(values)
            turned = values * cosine + jnp.where(first_half(values.shape), -swapped, swapped) * sine
            if step < QUERY_WIDTH // BLOCK:
                result = turned * SCALE
            else:
                lane = lax.broadcasted_iota(jnp.int32, values.shape, 1)
                result = jnp.where(lane % LANES < HEAD_SIZE, turned, values)
            out_ref[:, where] = result.astype(BF16)


def projections(chips, scaled, own, other, core, cosine, sine):
    tokens, width = scaled.shape
    block, columns = own.shape[0] // chips, own.shape[1]

    def whole(shape):
        return pl.BlockSpec(shape, lambda i: (0, 0))

    return pl.pallas_call(
        project_kernel,
        grid=(chips,),
        in_specs=[
            pl.BlockSpec(memory_space=pltpu.SMEM),
            whole((tokens, width)),
            pl.BlockSpec((block, columns), lambda i: (i, 0)),
            pl.BlockSpec((block, columns), lambda i: (i, 0)),
            whole((tokens, LANES)),
            whole((tokens, LANES)),
        ],
        out_specs=[whole((tokens, PROJECT)), whole((tokens, width)), whole((8, width))],
        out_shape=[
            jax.ShapeDtypeStruct((tokens, PROJECT), BF16),
            jax.ShapeDtypeStruct((tokens, width), BF16),
            jax.ShapeDtypeStruct((8, width), F32),
        ],
        scratch_shapes=[pltpu.VMEM((tokens, PROJECT), F32)],
        compiler_params=pltpu.CompilerParams(vmem_limit_bytes=VMEM_LIMIT),
        cost_estimate=NO_COST,
        name="project",
    )(core, scaled, own, other, cosine, sine)


def finish_residual(total_ref, extras, outs):
    tokens_ref, gain_ref = extras
    resid = tokens_ref[...].astype(F32) + total_ref[...]
    inverse = lax.rsqrt(jnp.mean(resid * resid, axis=1, keepdims=True) + EPSILON)
    outs[0][...] = resid
    outs[1][...] = (resid * inverse * gain_ref[...]).astype(BF16)


def finish_cast(total_ref, extras, outs):
    outs[0][...] = total_ref[...].astype(BF16)


def finish_input_grad(total_ref, extras, outs):
    d_resid_ref, tokens_ref, gain_ref = extras
    tokens = tokens_ref[...].astype(F32)
    inverse = lax.rsqrt(jnp.mean(tokens * tokens, axis=1, keepdims=True) + EPSILON)
    mixed = total_ref[...] * gain_ref[...]
    along = jnp.mean(mixed * tokens, axis=1, keepdims=True)
    grad = d_resid_ref[...] + inverse * mixed - tokens * (inverse * inverse * inverse) * along
    outs[0][...] = grad.astype(BF16)


def attend_kernel(query_ref, pair_ref, bias_ref, out_ref, log_ref):
    key, value = pair_ref[:, :HEAD_SIZE], pair_ref[:, HEAD_SIZE:]
    for two in range(GROUP // 2):
        parts = []
        for head in (2 * two, 2 * two + 1):
            query = query_ref[:, head * HEAD_SIZE : (head + 1) * HEAD_SIZE]
            scores = contract_last(key, query) + bias_ref[...]
            largest = jnp.max(scores, axis=0, keepdims=True)
            weights = jnp.exp(scores - largest)
            totals = jnp.sum(weights, axis=0, keepdims=True)
            parts.append(contract_rows(value, weights.astype(BF16)) / totals)
            log_ref[head : head + 1, :] = largest + jnp.log(totals)
        both = jnp.concatenate(parts, axis=0)
        out_ref[:, two * LANES : (two + 1) * LANES] = both.T.astype(BF16)


def attend(project, pairs, bias):
    tokens, keys = project.shape[0], pairs.shape[0]
    return pl.pallas_call(
        attend_kernel,
        grid=(KEY_VALUE_HEADS,),
        in_specs=[
            pl.BlockSpec((tokens, BLOCK), lambda i: (0, i)),
            pl.BlockSpec((keys, LANES), lambda i: (0, i)),
            pl.BlockSpec((keys, tokens), lambda i: (0, 0)),
        ],
        out_specs=[
            pl.BlockSpec((tokens, BLOCK), lambda i: (0, i)),
            pl.BlockSpec((GROUP, tokens), lambda i: (i, 0)),
        ],
        out_shape=[
            jax.ShapeDtypeStruct((tokens, QUERY_WIDTH), BF16),
            jax.ShapeDtypeStruct((HQ, tokens), F32),
        ],
        compiler_params=pltpu.CompilerParams(vmem_limit_bytes=VMEM_LIMIT),
        cost_estimate=cost(64 * HQ * tokens * keys * HEAD_SIZE),
        name="attend",
    )(project, pairs, bias)


def attend_back_kernel(
    query_ref, grad_ref, pair_ref, log_ref, bias_ref, cos_ref, sin_ref, d_query_ref, d_pair_ref
):
    key, value = pair_ref[:, :HEAD_SIZE], pair_ref[:, HEAD_SIZE:]
    d_key = jnp.zeros((key.shape[0], HEAD_SIZE), F32)
    d_value = jnp.zeros((key.shape[0], HEAD_SIZE), F32)
    for two in range(GROUP // 2):
        parts = []
        for head in (2 * two, 2 * two + 1):
            query = query_ref[:, head * HEAD_SIZE : (head + 1) * HEAD_SIZE]
            grad = grad_ref[:, head * HEAD_SIZE : (head + 1) * HEAD_SIZE]
            scores = contract_last(key, query) + bias_ref[...]
            probs = jnp.exp(scores - log_ref[head : head + 1, :])
            d_probs = contract_last(value, grad)
            row_dot = jnp.sum(probs * d_probs, axis=0, keepdims=True)
            d_scores = (probs * (d_probs - row_dot)).astype(BF16)
            d_value = d_value + jnp.dot(probs.astype(BF16), grad, preferred_element_type=F32)
            d_key = d_key + jnp.dot(d_scores, query, preferred_element_type=F32)
            parts.append(contract_rows(key, d_scores) * SCALE)
        both = jnp.concatenate(parts, axis=0).T.astype(BF16).astype(F32)
        swapped = half_swap(both * sin_ref[...])
        back = both * cos_ref[...] + jnp.where(first_half(both.shape), swapped, -swapped)
        d_query_ref[:, two * LANES : (two + 1) * LANES] = back.astype(BF16)
    d_pair_ref[...] = jnp.concatenate([d_key, d_value], axis=1)


def attend_back(project, grads, pairs, logs, bias, cosine, sine):
    tokens, keys = project.shape[0], pairs.shape[0]
    return pl.pallas_call(
        attend_back_kernel,
        grid=(KEY_VALUE_HEADS,),
        in_specs=[
            pl.BlockSpec((tokens, BLOCK), lambda i: (0, i)),
            pl.BlockSpec((tokens, BLOCK), lambda i: (0, i)),
            pl.BlockSpec((keys, LANES), lambda i: (0, i)),
            pl.BlockSpec((GROUP, tokens), lambda i: (i, 0)),
            pl.BlockSpec((keys, tokens), lambda i: (0, 0)),
            pl.BlockSpec((tokens, LANES), lambda i: (0, 0)),
            pl.BlockSpec((tokens, LANES), lambda i: (0, 0)),
        ],
        out_specs=[
            pl.BlockSpec((tokens, BLOCK), lambda i: (0, i)),
            pl.BlockSpec((keys, LANES), lambda i: (0, i)),
        ],
        out_shape=[
            jax.ShapeDtypeStruct((tokens, QUERY_WIDTH), BF16),
            jax.ShapeDtypeStruct((keys, 2 * KEY_WIDTH), F32),
        ],
        compiler_params=pltpu.CompilerParams(vmem_limit_bytes=VMEM_LIMIT),
        cost_estimate=cost(64 * HQ * tokens * keys * HEAD_SIZE),
        name="attend_back",
    )(project, grads, pairs, logs, bias, cosine, sine)


def load_rows(sources, held, sems):
    copies = []
    for (ref, first), to in zip(sources, held):
        for j in range(ref.shape[0]):
            part = ref.at[j, :, :, pl.ds(first, to.shape[3])]
            copies.append(pltpu.make_async_copy(part, to.at[:, j], sems.at[len(copies)]))
            copies[-1].start()
    for copy in copies:
        copy.wait()


def as_rows(ref):
    return ref[...].reshape(-1, ref.shape[3])


def ff_kernel(
    normed_ref, grad_ref, owned_ref, both_ref, down_ref, hidden_ref, d_gate_ref, d_up_ref, gate_w, up_w, down_w, sems
):
    @pl.when(pl.program_id(0) == 0)
    def _():
        load_rows([(both_ref, 0), (both_ref, gate_w.shape[3]), (down_ref, 0)], [gate_w, up_w, down_w], sems)

    normed, owned = normed_ref[...], owned_ref[...]
    gate = jnp.dot(normed, as_rows(gate_w), preferred_element_type=F32)
    up = jnp.dot(normed, as_rows(up_w), preferred_element_type=F32) * owned
    d_hidden = jnp.dot(grad_ref[...], as_rows(down_w), preferred_element_type=F32) * owned
    sigmoid_gate = jax.nn.sigmoid(gate)
    activated = gate * sigmoid_gate
    hidden_ref[...] = (activated * up).astype(BF16)
    d_gate = d_hidden * up * (sigmoid_gate * (1.0 + gate * (1.0 - sigmoid_gate)))
    d_gate_ref[...] = d_gate.astype(BF16)
    d_up_ref[...] = (d_hidden * activated).astype(BF16)


def feed_forward(normed, grads, owned, both, down):
    tokens, width = normed.shape
    sp_count, dp_count, rows, columns = down.shape
    block = min(tokens, 256)
    weight = pltpu.VMEM((dp_count, sp_count, rows, columns), BF16)
    return pl.pallas_call(
        ff_kernel,
        grid=(tokens // block,),
        in_specs=[
            pl.BlockSpec((block, width), lambda i: (i, 0)),
            pl.BlockSpec((block, width), lambda i: (i, 0)),
            pl.BlockSpec((1, columns), lambda i: (0, 0)),
            pl.BlockSpec(memory_space=pl.ANY),
            pl.BlockSpec(memory_space=pl.ANY),
        ],
        out_specs=[pl.BlockSpec((block, columns), lambda i: (i, 0))] * 3,
        out_shape=[jax.ShapeDtypeStruct((tokens, columns), BF16)] * 3,
        scratch_shapes=[weight, weight, weight, pltpu.SemaphoreType.DMA((3 * sp_count,))],
        compiler_params=pltpu.CompilerParams(vmem_limit_bytes=VMEM_LIMIT),
        cost_estimate=cost(10 * tokens * width * columns),
        name="feed_forward",
    )(normed, grads, owned, both, down)


def times_weights(values, weights):
    terms = len(values)
    count, columns = values[0].shape
    sp_count, dp_count, rows, _ = weights[0][0].shape
    width = sp_count * dp_count * rows
    block = min(count, 256)

    def kernel(*refs):
        value_refs, weight_refs = refs[:terms], refs[terms : 2 * terms]
        out_ref, held, sems = refs[2 * terms], refs[2 * terms + 1 : -1], refs[-1]

        @pl.when(pl.program_id(0) == 0)
        def _():
            load_rows([(r, w[1]) for r, w in zip(weight_refs, weights)], held, sems)

        total = contract_last(value_refs[0][...], as_rows(held[0]))
        for ref, weight in zip(value_refs[1:], held[1:]):
            total = total + contract_last(ref[...], as_rows(weight))
        out_ref[...] = total.astype(BF16)

    return pl.pallas_call(
        kernel,
        grid=(count // block,),
        in_specs=[pl.BlockSpec((block, columns), lambda i: (i, 0))] * terms
        + [pl.BlockSpec(memory_space=pl.ANY)] * terms,
        out_specs=pl.BlockSpec((block, width), lambda i: (i, 0)),
        out_shape=jax.ShapeDtypeStruct((count, width), BF16),
        scratch_shapes=[pltpu.VMEM((dp_count, sp_count, rows, columns), BF16)] * terms
        + [pltpu.SemaphoreType.DMA((terms * sp_count,))],
        compiler_params=pltpu.CompilerParams(vmem_limit_bytes=VMEM_LIMIT),
        cost_estimate=cost(4 * terms * count * width * columns),
        name="times_weights",
    )(*values, *(w[0] for w in weights))


def weight_grad(lefts, rights, sp_count, dp_count):
    tokens, width = lefts[0].shape
    columns = rights[0].shape[1]
    block = width // dp_count
    rows = block // sp_count

    def kernel(left_ref, left2_ref, right_ref, right2_ref, out_ref):
        total = contract_rows(left_ref[...], right_ref[...])
        total = total + contract_rows(left2_ref[...], right2_ref[...])
        out_ref[...] = total.astype(BF16).reshape(sp_count, 1, rows, columns)

    return pl.pallas_call(
        kernel,
        grid=(dp_count,),
        in_specs=[pl.BlockSpec((tokens, block), lambda i: (0, i))] * 2
        + [pl.BlockSpec((tokens, columns), lambda i: (0, 0))] * 2,
        out_specs=pl.BlockSpec((sp_count, 1, rows, columns), lambda i: (0, i, 0, 0)),
        out_shape=jax.ShapeDtypeStruct((sp_count, dp_count, rows, columns), BF16),
        compiler_params=pltpu.CompilerParams(vmem_limit_bytes=VMEM_LIMIT),
        cost_estimate=cost(8 * tokens * width * columns),
        name="weight_grad",
    )(*lefts, *rights).reshape(width, columns)


def assemble(pieces, starts, first=0, columns=None, deps=()):
    count = len(pieces)
    total = sum(piece.shape[0] for piece in pieces)
    columns = columns or pieces[0].shape[1]

    def kernel(starts_ref, *refs):
        out_ref, held, in_sems, out_sems = refs[count + len(deps) :]
        inward, outward = [], []
        for i in range(count):
            place = pl.ds(pl.multiple_of(starts_ref[i], 32), pieces[i].shape[0])
            piece = refs[i].at[:, pl.ds(first, columns)]
            inward.append(pltpu.make_async_copy(piece, held.at[place, :], in_sems.at[i]))
            outward.append(
                pltpu.make_async_copy(held.at[place, :], out_ref.at[place, :], out_sems.at[i])
            )
            inward[-1].start()
        for i in range(count):
            inward[i].wait()
            outward[i].start()
        for copy in outward:
            copy.wait()

    return pl.pallas_call(
        kernel,
        in_specs=[pl.BlockSpec(memory_space=pltpu.SMEM)]
        + [pl.BlockSpec(memory_space=pl.ANY)] * (count + len(deps)),
        out_specs=pl.BlockSpec(memory_space=pl.ANY),
        out_shape=jax.ShapeDtypeStruct((total, columns), pieces[0].dtype),
        scratch_shapes=[
            pltpu.VMEM((total, columns), pieces[0].dtype),
            pltpu.SemaphoreType.DMA((count,)),
            pltpu.SemaphoreType.DMA((count,)),
        ],
        compiler_params=pltpu.CompilerParams(vmem_limit_bytes=VMEM_LIMIT),
        cost_estimate=NO_COST,
        name="assemble",
    )(jnp.stack([jnp.asarray(s, jnp.int32) for s in starts]), *pieces, *deps)


def windows(arrays, starts, sizes, deps=()):
    count, rows, total = len(starts), arrays[0].shape[0], sum(sizes)

    def kernel(*refs):
        out_ref = refs[-1]
        for k in range(count):
            at = 0
            for i, size in enumerate(sizes):
                out_ref[k * rows : (k + 1) * rows, at : at + size] = refs[i][:, starts[k][i] : starts[k][i] + size]
                at += size

    return pl.pallas_call(
        kernel,
        in_specs=[pl.BlockSpec(memory_space=pltpu.VMEM)] * len(arrays)
        + [pl.BlockSpec(memory_space=pl.ANY)] * len(deps),
        out_specs=pl.BlockSpec(memory_space=pltpu.VMEM),
        out_shape=jax.ShapeDtypeStruct((count * rows, total), arrays[0].dtype),
        compiler_params=pltpu.CompilerParams(vmem_limit_bytes=VMEM_LIMIT),
        cost_estimate=NO_COST,
        name="windows",
    )(*arrays, *deps)


def after(value, *others):
    def kernel(*refs):
        del refs

    return pl.pallas_call(
        kernel,
        in_specs=[pl.BlockSpec(memory_space=pl.ANY)] * (1 + len(others)),
        out_specs=pl.BlockSpec(memory_space=pl.ANY),
        out_shape=jax.ShapeDtypeStruct(value.shape, value.dtype),
        input_output_aliases={0: 0},
        cost_estimate=NO_COST,
        name="after",
    )(value, *others)


def spread(value, axis, *others):
    count, rows = lax.axis_size(axis), value.shape[0]
    copies = jnp.broadcast_to(value[None], (count,) + value.shape).reshape(count * rows, -1)
    if others:
        copies = after(copies, *others)
    return lax.all_to_all(copies, axis, split_axis=0, concat_axis=0, tiled=True)


def sp_rows(value, sp_count, sp_index):
    rows = value.shape[0]
    pieces, starts = [value], [sp_index * rows]
    for j in range(1, sp_count):
        pieces.append(lax.ppermute(value, "sp", [(i, (i + j) % sp_count) for i in range(sp_count)]))
        starts.append((sp_index - j) % sp_count * rows)
    return assemble(pieces, starts)


def swap_cores(value):
    return lax.ppermute(value, "core", [(0, 1), (1, 0)])


def deal(value, axis):
    return lax.all_to_all(value, axis, split_axis=0, concat_axis=0, tiled=True)


def shift(value, count, by):
    pairs = [(i, i + by) for i in range(count) if 0 <= i + by < count]
    return lax.ppermute(value, "sp", pairs)


def local(
    inputs,
    cotangent,
    unit_lengths,
    attn_gain,
    w_query,
    key_weight,
    value_weight,
    w_output,
    mlp_gain,
    w_gate,
    w_up,
    w_down,
):
    chips = lax.axis_size("chip")
    dp_count = 2 * chips
    sp_count = lax.axis_size("sp")
    core = lax.axis_index("core")
    member = lax.axis_index("chip") * 2 + core
    core_only = core.astype(jnp.int32)[None]
    sp_index = lax.axis_index("sp")
    shard = inputs.shape[1]
    width = inputs.shape[2]
    length = shard * sp_count
    rows = w_query.shape[0]
    ff = w_gate.shape[1]
    query_local = QUERY_WIDTH // dp_count
    heads = range(KEY_VALUE_HEADS)
    members = range(dp_count)

    def head_columns(array, head):
        return array[:, head * HEAD_SIZE : (head + 1) * HEAD_SIZE]

    tiles = ff // LANES
    first = [tiles * m // dp_count for m in range(dp_count + 1)]
    window = max(b - a for a, b in zip(first, first[1:]))
    ff_local = window * LANES
    begin = [min(f, tiles - window) for f in first[:-1]]

    pair_columns = [head_columns(w, h) for h in heads for w in (key_weight, value_weight)]
    gains_local = jnp.pad(jnp.stack([attn_gain, mlp_gain], axis=1), ((0, 0), (0, LANES - 2)))
    in_local = jnp.concatenate([w_query] + pair_columns + [gains_local], axis=1)
    in_group = sp_rows(in_local, sp_count, sp_index)
    ff_mine = deal(
        windows([w_gate, w_up, w_down], [[b * LANES] * 3 for b in begin], [ff_local] * 3), MEMBERS
    )

    def along_sp(mine):
        return lax.all_gather(mine, "sp", axis=0).reshape(sp_count, dp_count, rows, mine.shape[1])

    both_mine, down_mine = ff_mine[:, : 2 * ff_local], ff_mine[:, 2 * ff_local :]
    down_weight = along_sp(after(down_mine, in_group))
    out_group = sp_rows(w_output, sp_count, sp_index)
    in_own = after(spread(in_group, "chip", ff_mine), out_group)
    in_other = swap_cores(in_own)
    out_own = spread(out_group, "chip", in_own, down_weight)
    both_weight = along_sp(after(both_mine, down_weight))
    tile = jnp.arange(ff_local, dtype=jnp.int32) // LANES + jnp.minimum(tiles * member // dp_count, tiles - window)
    owned = (tile >= tiles * member // dp_count) & (tile < tiles * (member + 1) // dp_count)
    owned = owned.astype(F32)[None]

    places = sp_index * shard + jnp.arange(shard, dtype=jnp.int32)
    begins = doc_layout(unit_lengths[0], places)
    cosine, sine = rope_tables(places - begins)
    pieces = key_pieces(length, shard, unit_lengths.shape[1])
    key_places = jnp.concatenate([places - j * shard for j in range(pieces)])[:, None]
    bias = jnp.where((key_places <= places[None]) & (key_places >= begins[None]), 0.0, MASKED)
    tokens_in = inputs[0].astype(F32)
    inv_one = lax.rsqrt(jnp.mean(tokens_in * tokens_in, axis=1, keepdims=True) + EPSILON)
    project, normed_one, gains = projections(
        chips, tokens_in * inv_one, in_own, in_other, core_only, cosine, sine
    )
    gain_one, gain_two = gains[:1], gains[1:2]
    pair = project[:, QUERY_WIDTH:]
    pairs = jnp.concatenate([pair] + [shift(pair, sp_count, j) for j in range(1, pieces)], axis=0)
    out_own = after(out_own, pairs)
    out_other = swap_cores(out_own)
    grad_own = spread(cotangent[0], "chip", out_own)
    grad_other = swap_cores(grad_own)
    attended, logs = attend(project, after(pairs, out_own), bias)
    resid, normed_two = member_product(
        False, chips, attended, out_own, out_other, core_only, [inputs[0], gain_two],
        [jax.ShapeDtypeStruct((shard, width), F32), jax.ShapeDtypeStruct((shard, width), BF16)],
        finish_residual, "out_project",
    )

    two_own = spread(normed_two, "chip", grad_own)
    two_other = swap_cores(two_own)
    normed_own = spread(normed_one, "chip", two_own)
    normed_other = swap_cores(normed_own)
    attended_own = spread(attended, "chip", normed_own)
    attended_other = swap_cores(attended_own)
    hidden_own, d_gate_own, d_up_own = feed_forward(two_own, grad_own, owned, both_weight, down_weight)
    hidden_other, d_gate_other, d_up_other = feed_forward(
        two_other, grad_other, owned, both_weight, down_weight
    )

    def for_sp(lefts, rights):
        return weight_grad(lefts, rights, sp_count, dp_count)

    def over_sp(total):
        return lax.psum_scatter(total, "sp", scatter_dimension=0, tiled=True)

    def chip_sums(own, other):
        return (own.astype(F32) + swap_cores(other).astype(F32)).astype(BF16)

    def plane_sum(sums, *others):
        arrived = after(deal(sums, "chip"), *others)
        return jnp.sum(arrived.reshape(chips, shard, width).astype(F32), axis=0)

    down_total = for_sp([grad_own, grad_other], [hidden_own, hidden_other])
    summed_down = over_sp(down_total)
    gate_and_up = [(both_weight, 0), (both_weight, ff_local)]
    d_gate_other = after(d_gate_other, down_total, normed_own)
    d_normed_other = times_weights([d_gate_other, d_up_other], gate_and_up)
    d_gate_own = after(d_gate_own, d_normed_other)
    d_normed_own = times_weights([d_gate_own, d_up_own], gate_and_up)
    d_gate_other = after(d_gate_other, d_normed_own)
    gate_total = for_sp([two_own, two_other], [d_gate_own, d_gate_other])
    summed_gate = over_sp(after(gate_total, summed_down))
    d_normed_sums = chip_sums(d_normed_own, d_normed_other)
    d_normed_sums = after(d_normed_sums, attended_own, summed_down)
    d_up_other = after(d_up_other, d_normed_sums)
    up_total = for_sp([two_own, two_other], [d_up_own, d_up_other])
    mlp_other = times_weights([after(hidden_other, up_total)], [(down_weight, 0)])
    mlp_own = times_weights([after(hidden_own, mlp_other)], [(down_weight, 0)])
    d_normed_two = plane_sum(d_normed_sums, mlp_own, summed_gate)

    inv_two = lax.rsqrt(jnp.mean(resid * resid, axis=1, keepdims=True) + EPSILON)
    mixed_two = d_normed_two * gain_two
    d_resid = (
        cotangent[0].astype(F32)
        + inv_two * mixed_two
        - resid * (inv_two * inv_two * inv_two) * jnp.mean(mixed_two * resid, axis=1, keepdims=True)
    )
    d_attn_out = d_resid.astype(BF16)

    def by_core(dealt):
        parts = dealt.reshape(chips, 2, shard, dealt.shape[1])
        return [
            lax.dynamic_index_in_dim(parts, c, 1, keepdims=False).reshape(chips * shard, -1)
            for c in (core, 1 - core)
        ]

    width_local = width // dp_count
    out_rows = deal(windows([d_attn_out], [[m * width_local] for m in members], [width_local]), MEMBERS)
    (d_attended,) = member_product(
        True, chips, d_attn_out, out_own, out_other, core_only, [],
        [jax.ShapeDtypeStruct((shard, QUERY_WIDTH), BF16)], finish_cast, "d_attended",
    )
    def to_owner(summed):
        return deal(summed, MEMBERS).reshape(dp_count, rows, summed.shape[1])

    back_down = to_owner(after(summed_down, out_rows))
    d_query, d_pairs = attend_back(project, after(d_attended, out_rows), pairs, logs, bias, cosine, sine)
    summed_up = over_sp(after(up_total, summed_gate))
    d_pair = d_pairs[:shard]
    for j in range(1, pieces):
        sent = d_pairs[j * shard : (j + 1) * shard].astype(BF16)
        d_pair = d_pair + shift(sent, sp_count, -j).astype(F32)
    d_pair = d_pair.astype(BF16).astype(F32)
    half_dim = HEAD_SIZE // 2
    unturned = []
    for head in heads:
        block = d_pair[:, head * LANES : (head + 1) * LANES]
        low, high = block[:, :half_dim], block[:, half_dim:HEAD_SIZE]
        c, s = cosine[:, :half_dim], sine[:, :half_dim]
        unturned += [low * c + high * s, high * c - low * s, block[:, HEAD_SIZE:]]
    d_pair = jnp.concatenate(unturned, axis=1).astype(BF16)
    back_gate = to_owner(after(summed_gate, back_down, d_query))
    out_parts = by_core(out_rows)
    out_total = contract_rows(out_parts[0], attended_own) + contract_rows(out_parts[1], attended_other)
    out_total = out_total.astype(BF16)
    summed_out = over_sp(after(out_total, summed_up))
    tile_of = [m * KEY_VALUE_HEADS // dp_count for m in members]
    project_columns = deal(
        windows(
            [d_query, d_pair],
            [[m * query_local, t * LANES] for m, t in zip(members, tile_of)],
            [query_local, LANES],
            [back_gate, out_total],
        ),
        MEMBERS,
    )
    (input_grad,) = member_product(
        False, chips, jnp.concatenate([d_query, d_pair], axis=1), in_own, in_other, core_only,
        [d_resid, inputs[0], gain_one],
        [jax.ShapeDtypeStruct((shard, width), BF16)], finish_input_grad, "input_grad",
    )

    grad_output_proj = summed_out.astype(F32)
    project_total = for_sp([normed_own, normed_other], by_core(project_columns))
    summed_project = over_sp(after(project_total, summed_out))
    mlp_sums = after(chip_sums(mlp_own, mlp_other), project_columns).reshape(chips, shard, width)
    chip = lax.axis_index("chip")
    mlp_parts = [lax.dynamic_index_in_dim(mlp_sums, chip, 0, keepdims=False)]
    for j in range(1, chips):
        sent = lax.dynamic_index_in_dim(mlp_sums, (chip + j) % chips, 0, keepdims=False)
        mlp_parts.append(lax.ppermute(sent, "chip", [(i, (i + j) % chips) for i in range(chips)]))
    output = (resid + sum(v.astype(F32) for v in mlp_parts)).astype(BF16)

    def ff_columns(back):
        parts = []
        for m in members:
            start = (first[m] - begin[m]) * LANES
            parts.append(back[m][:, start : start + (first[m + 1] - first[m]) * LANES])
        return jnp.concatenate(parts, axis=1).astype(F32)

    back_up = to_owner(after(summed_up, project_columns))
    grad_down, grad_gate, grad_up = (ff_columns(b) for b in (back_down, back_gate, back_up))
    back = to_owner(after(summed_project, back_up, output)).astype(F32)
    grad_query = jnp.concatenate([back[m][:, :query_local] for m in members], axis=1)
    pair_grads = [back[h * dp_count // KEY_VALUE_HEADS][:, query_local:] for h in heads]
    grad_key = jnp.concatenate([g[:, :HEAD_SIZE] for g in pair_grads], axis=1)
    grad_value = jnp.concatenate([g[:, HEAD_SIZE:] for g in pair_grads], axis=1)
    grad_attn_gain = (
        jnp.sum(w_query.astype(F32) * grad_query, axis=1)
        + jnp.sum(key_weight.astype(F32) * grad_key, axis=1)
        + jnp.sum(value_weight.astype(F32) * grad_value, axis=1)
    ) / attn_gain.astype(F32)
    grad_mlp_gain = (
        jnp.sum(w_gate.astype(F32) * grad_gate, axis=1) + jnp.sum(w_up.astype(F32) * grad_up, axis=1)
    ) / mlp_gain.astype(F32)
    return (
        output[None],
        input_grad[None],
        grad_attn_gain,
        grad_query,
        grad_key,
        grad_value,
        grad_output_proj,
        grad_mlp_gain,
        grad_gate,
        grad_up,
        grad_down,
    )


def solution(mesh):
    shape = (mesh.shape["dp"] // 2, 2, mesh.shape["sp"])
    cores = Mesh(mesh.devices.reshape(shape), EVERY)
    token_spec = P(MEMBERS, "sp", None)
    vector_spec = P(EVERY)
    weight_spec = P(EVERY, None)
    return jax.shard_map(
        local,
        mesh=cores,
        in_specs=(
            token_spec,
            token_spec,
            P(MEMBERS, None),
            vector_spec,
            weight_spec,
            weight_spec,
            weight_spec,
            weight_spec,
            vector_spec,
            weight_spec,
            weight_spec,
            weight_spec,
        ),
        out_specs=(
            token_spec,
            token_spec,
            vector_spec,
            weight_spec,
            weight_spec,
            weight_spec,
            weight_spec,
            vector_spec,
            weight_spec,
            weight_spec,
            weight_spec,
        ),
        check_vma=False,
    )
```

```python
import jax
import jax.numpy as jnp
from jax import lax
from jax.experimental import pallas as pl
from jax.experimental.pallas import tpu as pltpu
from jax.sharding import Mesh, PartitionSpec as P

HQ = 32
KEY_VALUE_HEADS = 4
HEAD_SIZE = 64
UNIT = 128
DOC_UNITS = 8
LANES = 128
GROUP = HQ // KEY_VALUE_HEADS
QUERY_WIDTH = HQ * HEAD_SIZE
KEY_WIDTH = KEY_VALUE_HEADS * HEAD_SIZE
PROJECT = QUERY_WIDTH + 2 * KEY_WIDTH
BLOCK = GROUP * HEAD_SIZE

EPSILON = 1e-05
MASKED = -1e30
SCALE = HEAD_SIZE ** (-0.5)
F32 = jnp.float32
BF16 = jnp.bfloat16
MEMBERS = ("chip", "core")
EVERY = ("chip", "core", "sp")
VMEM_LIMIT = 48 * 1024 * 1024
NO_COST = pl.CostEstimate(flops=0, bytes_accessed=0, transcendentals=0)


def cost(flops):
    return pl.CostEstimate(flops=int(flops), bytes_accessed=0, transcendentals=0)


def doc_layout(unit_lengths, places):
    token_lengths = unit_lengths * UNIT
    ends = jnp.cumsum(token_lengths)
    passed = places[:, None] >= ends[None, :]
    return jnp.sum(jnp.where(passed, token_lengths[None, :], 0), axis=1)


def rope_tables(positions):
    half_dim = HEAD_SIZE // 2
    inverse = jnp.power(10000.0, jnp.arange(half_dim, dtype=F32) * (-2.0 / HEAD_SIZE))
    angles = positions.astype(F32)[:, None] * inverse[None, :]
    return jnp.tile(jnp.cos(angles), (1, 4)), jnp.tile(jnp.sin(angles), (1, 4))


def key_pieces(length, shard, docs):
    units, per = length // UNIT, shard // UNIT
    longest = min(DOC_UNITS, units - 2)
    needed = 1
    for unit in range(units):
        earliest = max(0, unit - longest + 1)
        if docs == 2 and unit >= longest:
            earliest = max(earliest, units - longest)
        needed = max(needed, unit // per - earliest // per + 1)
    return needed


def contract_last(left, right):
    return lax.dot_general(left, right, (((1,), (1,)), ((), ())), preferred_element_type=F32)


def contract_rows(left, right):
    return lax.dot_general(left, right, (((0,), (0,)), ((), ())), preferred_element_type=F32)


def first_half(shape):
    lane = lax.broadcasted_iota(jnp.int32, shape, 1)
    return lane % HEAD_SIZE < HEAD_SIZE // 2


def half_swap(values):
    half_dim, lanes = HEAD_SIZE // 2, values.shape[1]
    return jnp.where(
        first_half(values.shape),
        pltpu.roll(values, lanes - half_dim, 1),
        pltpu.roll(values, half_dim, 1),
    )


def member_product(by_rows, chips, values, own, other, core, extras, out_shapes, finish, name):
    tokens = values.shape[0]
    block, columns = own.shape[0] // chips, own.shape[1]
    width = columns if by_rows else 2 * own.shape[0]

    def kernel(core_ref, values_ref, own_ref, other_ref, *refs):
        extra_refs, out_refs, total_ref = refs[: len(extras)], refs[len(extras) : -1], refs[-1]
        chip, mine = pl.program_id(0), core_ref[0]
        places = [
            pl.ds(pl.multiple_of((chip * 2 + c) * block, LANES), block) for c in (mine, 1 - mine)
        ]
        if by_rows:
            part = jnp.dot(values_ref[:, places[0]], own_ref[...], preferred_element_type=F32)
            part = part + jnp.dot(values_ref[:, places[1]], other_ref[...], preferred_element_type=F32)

            @pl.when(chip == 0)
            def _():
                total_ref[...] = part

            @pl.when(chip > 0)
            def _():
                total_ref[...] += part
        else:
            used = values_ref.shape[1]
            total_ref[:, places[0]] = contract_last(values_ref[...], own_ref[:, :used])
            total_ref[:, places[1]] = contract_last(values_ref[...], other_ref[:, :used])

        @pl.when(chip == chips - 1)
        def _():
            finish(total_ref, extra_refs, out_refs)

    def whole(shape):
        return pl.BlockSpec(shape, lambda i: (0,) * len(shape))

    return pl.pallas_call(
        kernel,
        grid=(chips,),
        in_specs=[
            pl.BlockSpec(memory_space=pltpu.SMEM),
            whole(values.shape),
            pl.BlockSpec((block, columns), lambda i: (i, 0)),
            pl.BlockSpec((block, columns), lambda i: (i, 0)),
        ]
        + [whole(e.shape) for e in extras],
        out_specs=[whole(o.shape) for o in out_shapes],
        out_shape=out_shapes,
        scratch_shapes=[pltpu.VMEM((tokens, width), F32)],
        compiler_params=pltpu.CompilerParams(vmem_limit_bytes=VMEM_LIMIT),
        cost_estimate=NO_COST,
        name=name,
    )(core, values, own, other, *extras)


def project_kernel(
    core_ref, scaled_ref, own_ref, other_ref, cos_ref, sin_ref, out_ref, normed_ref, gains_ref, total_ref
):
    chip, mine = pl.program_id(0), core_ref[0]
    block = own_ref.shape[0]
    part = None
    for ref, c in ((own_ref, mine), (other_ref, 1 - mine)):
        place = pl.ds(pl.multiple_of((chip * 2 + c) * block, LANES), block)
        gains = ref[:, PROJECT : PROJECT + LANES].astype(F32).T[:8]
        gains_ref[:, place] = gains
        normed = (scaled_ref[:, place] * gains[:1]).astype(BF16)
        normed_ref[:, place] = normed
        term = jnp.dot(normed, ref[:, :PROJECT], preferred_element_type=F32)
        part = term if part is None else part + term

    @pl.when(chip == 0)
    def _():
        total_ref[...] = part

    @pl.when(chip > 0)
    def _():
        total_ref[...] += part

    @pl.when(chip == pl.num_programs(0) - 1)
    def _():
        cosine = jnp.concatenate([cos_ref[...]] * (BLOCK // LANES), axis=1)
        sine = jnp.concatenate([sin_ref[...]] * (BLOCK // LANES), axis=1)
        for step in range(PROJECT // BLOCK):
            where = slice(step * BLOCK, (step + 1) * BLOCK)
            values = total_ref[:, where]
            swapped = half_swap(values)
            turned = values * cosine + jnp.where(first_half(values.shape), -swapped, swapped) * sine
            if step < QUERY_WIDTH // BLOCK:
                result = turned * SCALE
            else:
                lane = lax.broadcasted_iota(jnp.int32, values.shape, 1)
                result = jnp.where(lane % LANES < HEAD_SIZE, turned, values)
            out_ref[:, where] = result.astype(BF16)


def projections(chips, scaled, own, other, core, cosine, sine):
    tokens, width = scaled.shape
    block, columns = own.shape[0] // chips, own.shape[1]

    def whole(shape):
        return pl.BlockSpec(shape, lambda i: (0, 0))

    return pl.pallas_call(
        project_kernel,
        grid=(chips,),
        in_specs=[
            pl.BlockSpec(memory_space=pltpu.SMEM),
            whole((tokens, width)),
            pl.BlockSpec((block, columns), lambda i: (i, 0)),
            pl.BlockSpec((block, columns), lambda i: (i, 0)),
            whole((tokens, LANES)),
            whole((tokens, LANES)),
        ],
        out_specs=[whole((tokens, PROJECT)), whole((tokens, width)), whole((8, width))],
        out_shape=[
            jax.ShapeDtypeStruct((tokens, PROJECT), BF16),
            jax.ShapeDtypeStruct((tokens, width), BF16),
            jax.ShapeDtypeStruct((8, width), F32),
        ],
        scratch_shapes=[pltpu.VMEM((tokens, PROJECT), F32)],
        compiler_params=pltpu.CompilerParams(vmem_limit_bytes=VMEM_LIMIT),
        cost_estimate=NO_COST,
        name="project",
    )(core, scaled, own, other, cosine, sine)


def finish_residual(total_ref, extras, outs):
    tokens_ref, gain_ref = extras
    resid = tokens_ref[...].astype(F32) + total_ref[...]
    inverse = lax.rsqrt(jnp.mean(resid * resid, axis=1, keepdims=True) + EPSILON)
    outs[0][...] = resid
    outs[1][...] = (resid * inverse * gain_ref[...]).astype(BF16)


def finish_cast(total_ref, extras, outs):
    outs[0][...] = total_ref[...].astype(BF16)


def finish_input_grad(total_ref, extras, outs):
    d_resid_ref, tokens_ref, gain_ref = extras
    tokens = tokens_ref[...].astype(F32)
    inverse = lax.rsqrt(jnp.mean(tokens * tokens, axis=1, keepdims=True) + EPSILON)
    mixed = total_ref[...] * gain_ref[...]
    along = jnp.mean(mixed * tokens, axis=1, keepdims=True)
    grad = d_resid_ref[...] + inverse * mixed - tokens * (inverse * inverse * inverse) * along
    outs[0][...] = grad.astype(BF16)


def attend_kernel(query_ref, pair_ref, bias_ref, out_ref, log_ref):
    key, value = pair_ref[:, :HEAD_SIZE], pair_ref[:, HEAD_SIZE:]
    for two in range(GROUP // 2):
        parts = []
        for head in (2 * two, 2 * two + 1):
            query = query_ref[:, head * HEAD_SIZE : (head + 1) * HEAD_SIZE]
            scores = contract_last(key, query) + bias_ref[...]
            largest = jnp.max(scores, axis=0, keepdims=True)
            weights = jnp.exp(scores - largest)
            totals = jnp.sum(weights, axis=0, keepdims=True)
            parts.append(contract_rows(value, weights.astype(BF16)) / totals)
            log_ref[head : head + 1, :] = largest + jnp.log(totals)
        both = jnp.concatenate(parts, axis=0)
        out_ref[:, two * LANES : (two + 1) * LANES] = both.T.astype(BF16)


def attend(project, pairs, bias):
    tokens, keys = project.shape[0], pairs.shape[0]
    return pl.pallas_call(
        attend_kernel,
        grid=(KEY_VALUE_HEADS,),
        in_specs=[
            pl.BlockSpec((tokens, BLOCK), lambda i: (0, i)),
            pl.BlockSpec((keys, LANES), lambda i: (0, i)),
            pl.BlockSpec((keys, tokens), lambda i: (0, 0)),
        ],
        out_specs=[
            pl.BlockSpec((tokens, BLOCK), lambda i: (0, i)),
            pl.BlockSpec((GROUP, tokens), lambda i: (i, 0)),
        ],
        out_shape=[
            jax.ShapeDtypeStruct((tokens, QUERY_WIDTH), BF16),
            jax.ShapeDtypeStruct((HQ, tokens), F32),
        ],
        compiler_params=pltpu.CompilerParams(vmem_limit_bytes=VMEM_LIMIT),
        cost_estimate=NO_COST,
        name="attend",
    )(project, pairs, bias)


def attend_back_kernel(
    query_ref, grad_ref, pair_ref, log_ref, bias_ref, cos_ref, sin_ref, d_query_ref, *d_pair_refs
):
    key, value = pair_ref[:, :HEAD_SIZE], pair_ref[:, HEAD_SIZE:]
    d_key = jnp.zeros((key.shape[0], HEAD_SIZE), F32)
    d_value = jnp.zeros((key.shape[0], HEAD_SIZE), F32)
    for two in range(GROUP // 2):
        parts = []
        for head in (2 * two, 2 * two + 1):
            query = query_ref[:, head * HEAD_SIZE : (head + 1) * HEAD_SIZE]
            grad = grad_ref[:, head * HEAD_SIZE : (head + 1) * HEAD_SIZE]
            scores = contract_last(key, query) + bias_ref[...]
            probs = jnp.exp(scores - log_ref[head : head + 1, :])
            d_probs = contract_last(value, grad)
            row_dot = jnp.sum(probs * d_probs, axis=0, keepdims=True)
            d_scores = (probs * (d_probs - row_dot)).astype(BF16)
            d_value = d_value + jnp.dot(probs.astype(BF16), grad, preferred_element_type=F32)
            d_key = d_key + jnp.dot(d_scores, query, preferred_element_type=F32)
            parts.append(contract_rows(key, d_scores) * SCALE)
        both = jnp.concatenate(parts, axis=0).T.astype(BF16).astype(F32)
        swapped = half_swap(both * sin_ref[...])
        back = both * cos_ref[...] + jnp.where(first_half(both.shape), swapped, -swapped)
        d_query_ref[:, two * LANES : (two + 1) * LANES] = back.astype(BF16)
    d_pair = jnp.concatenate([d_key, d_value], axis=1)
    shard = query_ref.shape[0]
    for piece, ref in enumerate(d_pair_refs):
        ref[...] = d_pair[piece * shard : (piece + 1) * shard].astype(ref.dtype)


def attend_back(project, grads, pairs, logs, bias, cosine, sine):
    tokens, keys = project.shape[0], pairs.shape[0]
    return pl.pallas_call(
        attend_back_kernel,
        grid=(KEY_VALUE_HEADS,),
        in_specs=[
            pl.BlockSpec((tokens, BLOCK), lambda i: (0, i)),
            pl.BlockSpec((tokens, BLOCK), lambda i: (0, i)),
            pl.BlockSpec((keys, LANES), lambda i: (0, i)),
            pl.BlockSpec((GROUP, tokens), lambda i: (i, 0)),
            pl.BlockSpec((keys, tokens), lambda i: (0, 0)),
            pl.BlockSpec((tokens, LANES), lambda i: (0, 0)),
            pl.BlockSpec((tokens, LANES), lambda i: (0, 0)),
        ],
        out_specs=[
            pl.BlockSpec((tokens, BLOCK), lambda i: (0, i)),
        ]
        + [pl.BlockSpec((tokens, LANES), lambda i: (0, i))] * (keys // tokens),
        out_shape=[
            jax.ShapeDtypeStruct((tokens, QUERY_WIDTH), BF16),
            jax.ShapeDtypeStruct((tokens, 2 * KEY_WIDTH), F32),
        ]
        + [jax.ShapeDtypeStruct((tokens, 2 * KEY_WIDTH), BF16)] * (keys // tokens - 1),
        compiler_params=pltpu.CompilerParams(vmem_limit_bytes=VMEM_LIMIT),
        cost_estimate=cost(64 * HQ * tokens * keys * HEAD_SIZE),
        name="attend_back",
    )(project, grads, pairs, logs, bias, cosine, sine)


def load_rows(sources, held, sems):
    copies = []
    for (ref, first), to in zip(sources, held):
        for j in range(ref.shape[0]):
            part = ref.at[j, :, :, pl.ds(first, to.shape[3])]
            copies.append(pltpu.make_async_copy(part, to.at[:, j], sems.at[len(copies)]))
            copies[-1].start()
    for copy in copies:
        copy.wait()


def as_rows(ref):
    return ref[...].reshape(-1, ref.shape[3])


def ff_kernel(normed_ref, grad_ref, owned_ref, weight_ref, hidden_ref, d_gate_ref, d_up_ref, *held):
    (gate_w, up_w, down_w), sems = held[:3], held[3]
    columns = gate_w.shape[3]

    @pl.when(pl.program_id(0) == 0)
    def _():
        load_rows([(weight_ref, i * columns) for i in range(3)], [gate_w, up_w, down_w], sems)

    normed, owned = normed_ref[...], owned_ref[...]
    gate = jnp.dot(normed, as_rows(gate_w), preferred_element_type=F32)
    up = jnp.dot(normed, as_rows(up_w), preferred_element_type=F32) * owned
    d_hidden = jnp.dot(grad_ref[...], as_rows(down_w), preferred_element_type=F32) * owned
    sigmoid_gate = jax.nn.sigmoid(gate)
    activated = gate * sigmoid_gate
    hidden_ref[...] = (activated * up).astype(BF16)
    d_gate = d_hidden * up * (sigmoid_gate * (1.0 + gate * (1.0 - sigmoid_gate)))
    d_gate_ref[...] = d_gate.astype(BF16)
    d_up_ref[...] = (d_hidden * activated).astype(BF16)


def feed_forward(normed, grads, owned, weight, columns):
    tokens, width = normed.shape
    sp_count, dp_count, rows, _ = weight.shape
    block = min(tokens, 256)
    held = pltpu.VMEM((dp_count, sp_count, rows, columns), BF16)
    return pl.pallas_call(
        ff_kernel,
        grid=(tokens // block,),
        in_specs=[
            pl.BlockSpec((block, width), lambda i: (i, 0)),
            pl.BlockSpec((block, width), lambda i: (i, 0)),
            pl.BlockSpec((1, columns), lambda i: (0, 0)),
            pl.BlockSpec(memory_space=pl.ANY),
        ],
        out_specs=[pl.BlockSpec((block, columns), lambda i: (i, 0))] * 3,
        out_shape=[jax.ShapeDtypeStruct((tokens, columns), BF16)] * 3,
        scratch_shapes=[held, held, held, pltpu.SemaphoreType.DMA((3 * sp_count,))],
        compiler_params=pltpu.CompilerParams(vmem_limit_bytes=VMEM_LIMIT),
        cost_estimate=NO_COST,
        name="feed_forward",
    )(normed, grads, owned, weight)


def times_weights(values, weights):
    terms = len(values)
    count, columns = values[0].shape
    sp_count, dp_count, rows, _ = weights[0][0].shape
    width = sp_count * dp_count * rows
    block = min(count, 256)

    def kernel(*refs):
        value_refs, weight_refs = refs[:terms], refs[terms : 2 * terms]
        out_ref, held, sems = refs[2 * terms], refs[2 * terms + 1 : -1], refs[-1]

        @pl.when(pl.program_id(0) == 0)
        def _():
            load_rows([(r, w[1]) for r, w in zip(weight_refs, weights)], held, sems)

        total = contract_last(value_refs[0][...], as_rows(held[0]))
        for ref, weight in zip(value_refs[1:], held[1:]):
            total = total + contract_last(ref[...], as_rows(weight))
        out_ref[...] = total.astype(BF16)

    return pl.pallas_call(
        kernel,
        grid=(count // block,),
        in_specs=[pl.BlockSpec((block, columns), lambda i: (i, 0))] * terms
        + [pl.BlockSpec(memory_space=pl.ANY)] * terms,
        out_specs=pl.BlockSpec((block, width), lambda i: (i, 0)),
        out_shape=jax.ShapeDtypeStruct((count, width), BF16),
        scratch_shapes=[pltpu.VMEM((dp_count, sp_count, rows, columns), BF16)] * terms
        + [pltpu.SemaphoreType.DMA((terms * sp_count,))],
        compiler_params=pltpu.CompilerParams(vmem_limit_bytes=VMEM_LIMIT),
        cost_estimate=NO_COST,
        name="times_weights",
    )(*values, *(w[0] for w in weights))


def row_grad(dealt, rights, core, chips):
    tokens, columns = rights[0].shape
    rows = dealt.shape[1]
    block = min(columns, 512)

    def kernel(core_ref, left_ref, left2_ref, right_ref, right2_ref, out_ref):
        total = contract_rows(left_ref[...].reshape(tokens, rows), right_ref[...])
        total = total + contract_rows(left2_ref[...].reshape(tokens, rows), right2_ref[...])
        out_ref[...] = total.astype(BF16)

    dealt = dealt.reshape(chips, 2, tokens // chips, rows)
    part = (chips, 1, tokens // chips, rows)
    return pl.pallas_call(
        kernel,
        grid_spec=pltpu.PrefetchScalarGridSpec(
            num_scalar_prefetch=1,
            grid=(columns // block,),
            in_specs=[
                pl.BlockSpec(part, lambda i, c: (0, c[0], 0, 0)),
                pl.BlockSpec(part, lambda i, c: (0, 1 - c[0], 0, 0)),
                pl.BlockSpec((tokens, block), lambda i, c: (0, i)),
                pl.BlockSpec((tokens, block), lambda i, c: (0, i)),
            ],
            out_specs=pl.BlockSpec((rows, block), lambda i, c: (0, i)),
        ),
        out_shape=jax.ShapeDtypeStruct((rows, columns), BF16),
        compiler_params=pltpu.CompilerParams(vmem_limit_bytes=VMEM_LIMIT),
        cost_estimate=NO_COST,
        name="row_grad",
    )(core, dealt, dealt, *rights)


def dealt_grad(lefts, dealt, width, sp_count, dp_count, core):
    tokens = lefts[0].shape[0]
    columns = dealt.shape[1]
    block = width // dp_count
    rows = block // sp_count
    chips = dp_count // 2

    def kernel(core_ref, left_ref, left2_ref, right_ref, right2_ref, out_ref, done_ref):
        total = contract_rows(left_ref[...], right_ref[...].reshape(tokens, columns))
        total = total + contract_rows(left2_ref[...], right2_ref[...].reshape(tokens, columns))
        out_ref[...] = total.astype(BF16).reshape(sp_count, 1, rows, columns)
        done_ref[...] = jnp.zeros_like(done_ref)

    dealt = dealt.reshape(chips, 2, tokens // chips, columns)
    part = (chips, 1, tokens // chips, columns)
    total, done = pl.pallas_call(
        kernel,
        grid_spec=pltpu.PrefetchScalarGridSpec(
            num_scalar_prefetch=1,
            grid=(dp_count,),
            in_specs=[
                pl.BlockSpec((tokens, block), lambda i, c: (0, i)),
                pl.BlockSpec((tokens, block), lambda i, c: (0, i)),
                pl.BlockSpec(part, lambda i, c: (0, c[0], 0, 0)),
                pl.BlockSpec(part, lambda i, c: (0, 1 - c[0], 0, 0)),
            ],
            out_specs=[
                pl.BlockSpec((sp_count, 1, rows, columns), lambda i, c: (0, i, 0, 0)),
                pl.BlockSpec((8, LANES), lambda i, c: (0, 0)),
            ],
        ),
        out_shape=[
            jax.ShapeDtypeStruct((sp_count, dp_count, rows, columns), BF16),
            jax.ShapeDtypeStruct((8, LANES), F32),
        ],
        compiler_params=pltpu.CompilerParams(vmem_limit_bytes=VMEM_LIMIT),
        cost_estimate=NO_COST,
        name="dealt_grad",
    )(core, *lefts, dealt, dealt)
    return total.reshape(width, columns), done


def weight_grad(lefts, rights, width, sp_count, dp_count):
    tokens = lefts[0].shape[0]
    columns = rights[0].shape[1]
    block = width // dp_count
    rows = block // sp_count

    def kernel(left_ref, left2_ref, right_ref, right2_ref, out_ref, done_ref):
        total = contract_rows(left_ref[...], right_ref[...])
        total = total + contract_rows(left2_ref[...], right2_ref[...])
        out_ref[...] = total.astype(BF16).reshape(sp_count, 1, rows, columns)
        done_ref[...] = jnp.zeros_like(done_ref)

    total, done = pl.pallas_call(
        kernel,
        grid=(dp_count,),
        in_specs=[pl.BlockSpec((tokens, block), lambda i: (0, i))] * 2
        + [pl.BlockSpec((tokens, columns), lambda i: (0, 0))] * 2,
        out_specs=[
            pl.BlockSpec((sp_count, 1, rows, columns), lambda i: (0, i, 0, 0)),
            pl.BlockSpec((8, LANES), lambda i: (0, 0)),
        ],
        out_shape=[
            jax.ShapeDtypeStruct((sp_count, dp_count, rows, columns), BF16),
            jax.ShapeDtypeStruct((8, LANES), F32),
        ],
        compiler_params=pltpu.CompilerParams(vmem_limit_bytes=VMEM_LIMIT),
        cost_estimate=NO_COST,
        name="weight_grad",
    )(*lefts, *rights)
    return total.reshape(width, columns), done


def assemble(pieces, starts, first=0, columns=None, deps=()):
    count = len(pieces)
    total = sum(piece.shape[0] for piece in pieces)
    columns = columns or pieces[0].shape[1]

    def kernel(starts_ref, *refs):
        out_ref, held, in_sems, out_sems = refs[count + len(deps) :]
        inward, outward = [], []
        for i in range(count):
            place = pl.ds(pl.multiple_of(starts_ref[i], 32), pieces[i].shape[0])
            piece = refs[i].at[:, pl.ds(first, columns)]
            inward.append(pltpu.make_async_copy(piece, held.at[place, :], in_sems.at[i]))
            outward.append(
                pltpu.make_async_copy(held.at[place, :], out_ref.at[place, :], out_sems.at[i])
            )
            inward[-1].start()
        for i in range(count):
            inward[i].wait()
            outward[i].start()
        for copy in outward:
            copy.wait()

    return pl.pallas_call(
        kernel,
        in_specs=[pl.BlockSpec(memory_space=pltpu.SMEM)]
        + [pl.BlockSpec(memory_space=pl.ANY)] * (count + len(deps)),
        out_specs=pl.BlockSpec(memory_space=pl.ANY),
        out_shape=jax.ShapeDtypeStruct((total, columns), pieces[0].dtype),
        scratch_shapes=[
            pltpu.VMEM((total, columns), pieces[0].dtype),
            pltpu.SemaphoreType.DMA((count,)),
            pltpu.SemaphoreType.DMA((count,)),
        ],
        compiler_params=pltpu.CompilerParams(vmem_limit_bytes=VMEM_LIMIT),
        cost_estimate=NO_COST,
        name="assemble",
    )(jnp.stack([jnp.asarray(s, jnp.int32) for s in starts]), *pieces, *deps)


def windows(arrays, starts, sizes, deps=()):
    count, rows, total = len(starts), arrays[0].shape[0], sum(sizes)

    def kernel(*refs):
        out_ref = refs[-1]
        for k in range(count):
            at = 0
            for i, size in enumerate(sizes):
                out_ref[k * rows : (k + 1) * rows, at : at + size] = refs[i][:, starts[k][i] : starts[k][i] + size]
                at += size

    return pl.pallas_call(
        kernel,
        in_specs=[pl.BlockSpec(memory_space=pltpu.VMEM)] * len(arrays)
        + [pl.BlockSpec(memory_space=pl.ANY)] * len(deps),
        out_specs=pl.BlockSpec(memory_space=pltpu.VMEM),
        out_shape=jax.ShapeDtypeStruct((count * rows, total), arrays[0].dtype),
        compiler_params=pltpu.CompilerParams(vmem_limit_bytes=VMEM_LIMIT),
        cost_estimate=NO_COST,
        name="windows",
    )(*arrays, *deps)


def summed(left, right):
    rows, columns = left.shape
    block = min(rows, 256)

    def kernel(left_ref, right_ref, out_ref):
        out_ref[...] = (left_ref[...].astype(F32) + right_ref[...].astype(F32)).astype(BF16)

    spec = pl.BlockSpec((block, columns), lambda i: (i, 0))
    return pl.pallas_call(
        kernel,
        grid=(rows // block,),
        in_specs=[spec] * 2,
        out_specs=spec,
        out_shape=jax.ShapeDtypeStruct(left.shape, BF16),
        cost_estimate=NO_COST,
        compiler_params=pltpu.CompilerParams(vmem_limit_bytes=VMEM_LIMIT),
        name="summed",
    )(left, right)


def residual_grad(arrived, grads, resid, gain):
    chips, tokens, width = arrived.shape
    block = min(tokens, 64)

    def kernel(arrived_ref, grad_ref, resid_ref, gain_ref, d_resid_ref, rounded_ref):
        total = arrived_ref[0].astype(F32)
        for i in range(1, chips):
            total = total + arrived_ref[i].astype(F32)
        resid = resid_ref[...]
        inverse = lax.rsqrt(jnp.mean(resid * resid, axis=1, keepdims=True) + EPSILON)
        mixed = total * gain_ref[...]
        along = jnp.mean(mixed * resid, axis=1, keepdims=True)
        d_resid = grad_ref[...].astype(F32) + inverse * mixed - resid * (inverse * inverse * inverse) * along
        d_resid_ref[...] = d_resid
        rounded_ref[...] = d_resid.astype(BF16)

    spec = pl.BlockSpec((block, width), lambda i: (i, 0))
    return pl.pallas_call(
        kernel,
        grid=(tokens // block,),
        in_specs=[
            pl.BlockSpec((chips, block, width), lambda i: (0, i, 0)),
            spec,
            spec,
            pl.BlockSpec((1, width), lambda i: (0, 0)),
        ],
        out_specs=[spec, spec],
        out_shape=[jax.ShapeDtypeStruct((tokens, width), F32), jax.ShapeDtypeStruct((tokens, width), BF16)],
        compiler_params=pltpu.CompilerParams(vmem_limit_bytes=VMEM_LIMIT),
        cost_estimate=NO_COST,
        name="residual_grad",
    )(arrived, grads, resid, gain)


def pair_back(own, arrived, cosine, sine):
    tokens, columns = own.shape
    count = len(arrived)

    def kernel(own_ref, cos_ref, sin_ref, *refs):
        total = own_ref[...]
        for ref in refs[:count]:
            total = total + ref[...].astype(F32)
        total = total.astype(BF16).astype(F32)
        times = columns // LANES
        cosine = jnp.concatenate([cos_ref[...]] * times, axis=1)
        sine = jnp.concatenate([sin_ref[...]] * times, axis=1)
        swapped = half_swap(total * sine)
        back = total * cosine + jnp.where(first_half(total.shape), swapped, -swapped)
        lane = lax.broadcasted_iota(jnp.int32, total.shape, 1)
        refs[count][...] = jnp.where(lane % LANES < HEAD_SIZE, back, total).astype(BF16)

    return pl.pallas_call(
        kernel,
        out_shape=jax.ShapeDtypeStruct((tokens, columns), BF16),
        compiler_params=pltpu.CompilerParams(vmem_limit_bytes=VMEM_LIMIT),
        cost_estimate=NO_COST,
        name="pair_back",
    )(own, cosine, sine, *arrived)


def after(value, *others):
    def kernel(*refs):
        del refs

    return pl.pallas_call(
        kernel,
        in_specs=[pl.BlockSpec(memory_space=pl.ANY)] * (1 + len(others)),
        out_specs=pl.BlockSpec(memory_space=pl.ANY),
        out_shape=jax.ShapeDtypeStruct(value.shape, value.dtype),
        input_output_aliases={0: 0},
        cost_estimate=NO_COST,
        name="after",
    )(value, *others)


def spread(value, axis, *others):
    count, rows = lax.axis_size(axis), value.shape[0]
    copies = jnp.broadcast_to(value[None], (count,) + value.shape).reshape(count * rows, -1)
    if others:
        copies = after(copies, *others)
    return lax.all_to_all(copies, axis, split_axis=0, concat_axis=0, tiled=True)


def sp_rows(value, sp_count, sp_index):
    rows = value.shape[0]
    pieces, starts = [value], [sp_index * rows]
    for j in range(1, sp_count):
        pieces.append(lax.ppermute(value, "sp", [(i, (i + j) % sp_count) for i in range(sp_count)]))
        starts.append((sp_index - j) % sp_count * rows)
    return assemble(pieces, starts)


def swap_cores(value):
    return lax.ppermute(value, "core", [(0, 1), (1, 0)])


def deal(value, axis):
    return lax.all_to_all(value, axis, split_axis=0, concat_axis=0, tiled=True)


def shift(value, count, by):
    pairs = [(i, i + by) for i in range(count) if 0 <= i + by < count]
    return lax.ppermute(value, "sp", pairs)


def local(
    inputs,
    cotangent,
    unit_lengths,
    attn_gain,
    w_query,
    key_weight,
    value_weight,
    w_output,
    mlp_gain,
    w_gate,
    w_up,
    w_down,
):
    chips = lax.axis_size("chip")
    dp_count = 2 * chips
    sp_count = lax.axis_size("sp")
    core = lax.axis_index("core")
    member = lax.axis_index("chip") * 2 + core
    core_only = core.astype(jnp.int32)[None]
    sp_index = lax.axis_index("sp")
    shard = inputs.shape[1]
    width = inputs.shape[2]
    length = shard * sp_count
    rows = w_query.shape[0]
    ff = w_gate.shape[1]
    query_local = QUERY_WIDTH // dp_count
    heads = range(KEY_VALUE_HEADS)
    members = range(dp_count)

    def head_columns(array, head):
        return array[:, head * HEAD_SIZE : (head + 1) * HEAD_SIZE]

    tiles = ff // LANES
    first = [tiles * m // dp_count for m in range(dp_count + 1)]
    window = max(b - a for a, b in zip(first, first[1:]))
    ff_local = window * LANES
    begin = [min(f, tiles - window) for f in first[:-1]]

    pair_columns = [head_columns(w, h) for h in heads for w in (key_weight, value_weight)]
    gains_local = jnp.pad(jnp.stack([attn_gain, mlp_gain], axis=1), ((0, 0), (0, LANES - 2)))
    in_local = jnp.concatenate([w_query] + pair_columns + [gains_local], axis=1)
    in_group = sp_rows(in_local, sp_count, sp_index)
    ff_mine = deal(
        windows([w_gate, w_up, w_down], [[b * LANES] * 3 for b in begin], [ff_local] * 3), MEMBERS
    )

    def along_sp(mine):
        return lax.all_gather(mine, "sp", axis=0).reshape(sp_count, dp_count, rows, mine.shape[1])

    out_group = sp_rows(w_output, sp_count, sp_index)
    ff_weight = along_sp(after(ff_mine, in_group))
    gate_weight, up_weight, down_weight = ((ff_weight, i * ff_local) for i in range(3))
    in_own = after(spread(in_group, "chip", ff_mine), out_group)
    in_other = swap_cores(in_own)
    out_own = spread(out_group, "chip", in_own)
    tile = jnp.arange(ff_local, dtype=jnp.int32) // LANES + jnp.minimum(tiles * member // dp_count, tiles - window)
    owned = (tile >= tiles * member // dp_count) & (tile < tiles * (member + 1) // dp_count)
    owned = owned.astype(F32)[None]

    places = sp_index * shard + jnp.arange(shard, dtype=jnp.int32)
    begins = doc_layout(unit_lengths[0], places)
    cosine, sine = rope_tables(places - begins)
    pieces = key_pieces(length, shard, unit_lengths.shape[1])
    key_places = jnp.concatenate([places - j * shard for j in range(pieces)])[:, None]
    bias = jnp.where((key_places <= places[None]) & (key_places >= begins[None]), 0.0, MASKED)
    tokens_in = inputs[0].astype(F32)
    inv_one = lax.rsqrt(jnp.mean(tokens_in * tokens_in, axis=1, keepdims=True) + EPSILON)
    project, normed_one, gains = projections(
        chips, tokens_in * inv_one, in_own, in_other, core_only, cosine, sine
    )
    gain_one, gain_two = gains[:1], gains[1:2]
    pair = project[:, QUERY_WIDTH:]
    pairs = jnp.concatenate([pair] + [shift(pair, sp_count, j) for j in range(1, pieces)], axis=0)
    out_own = after(out_own, pairs)
    out_other = swap_cores(out_own)
    grad_own = spread(cotangent[0], "chip", out_own)
    grad_other = swap_cores(grad_own)
    attended, logs = attend(project, after(pairs, out_own), bias)
    resid, normed_two = member_product(
        False, chips, attended, out_own, out_other, core_only, [inputs[0], gain_two],
        [jax.ShapeDtypeStruct((shard, width), F32), jax.ShapeDtypeStruct((shard, width), BF16)],
        finish_residual, "out_project",
    )

    two_own = spread(normed_two, "chip", grad_own, ff_weight)
    two_other = swap_cores(two_own)
    normed_own = spread(normed_one, "chip", two_own)
    normed_other = swap_cores(normed_own)
    attended_own = spread(attended, "chip", normed_own)
    attended_other = swap_cores(attended_own)
    hidden_own, d_gate_own, d_up_own = feed_forward(two_own, grad_own, owned, ff_weight, ff_local)
    hidden_other, d_gate_other, d_up_other = feed_forward(
        two_other, grad_other, owned, ff_weight, ff_local
    )

    def for_sp(lefts, rights):
        return weight_grad(lefts, rights, width, sp_count, dp_count)

    def over_sp(total):
        return lax.psum_scatter(total, "sp", scatter_dimension=0, tiled=True)

    def chip_sums(own, other):
        return summed(own, swap_cores(other))

    down_total, down_done = for_sp([grad_own, grad_other], [hidden_own, hidden_other])
    summed_down = over_sp(down_total)
    gate_and_up = [gate_weight, up_weight]
    d_gate_other = after(d_gate_other, down_total, normed_own)
    d_normed_other = times_weights([d_gate_other, d_up_other], gate_and_up)
    d_gate_own = after(d_gate_own, d_normed_other)
    d_normed_own = times_weights([d_gate_own, d_up_own], gate_and_up)
    d_normed_sums = after(chip_sums(d_normed_own, d_normed_other), attended_own)
    d_gate_other = after(d_gate_other, d_normed_sums)
    gate_total, gate_done = for_sp([two_own, two_other], [d_gate_own, d_gate_other])
    summed_gate = over_sp(after(gate_total, summed_down))
    mlp_other = times_weights([after(hidden_other, gate_done)], [down_weight])
    mlp_own = times_weights([after(hidden_own, mlp_other)], [down_weight])
    mlp_sums = chip_sums(mlp_own, mlp_other)
    d_up_other = after(d_up_other, mlp_sums)
    up_total, up_done = for_sp([two_own, two_other], [d_up_own, d_up_other])
    d_normed_two = after(deal(d_normed_sums, "chip"), up_done).reshape(chips, shard, width)
    d_resid, d_attn_out = residual_grad(d_normed_two, cotangent[0], resid, gain_two)

    width_local = width // dp_count
    out_rows = deal(windows([d_attn_out], [[m * width_local] for m in members], [width_local]), MEMBERS)
    (d_attended,) = member_product(
        True, chips, d_attn_out, out_own, out_other, core_only, [],
        [jax.ShapeDtypeStruct((shard, QUERY_WIDTH), BF16)], finish_cast, "d_attended",
    )
    def to_owner(summed):
        return deal(summed, MEMBERS).reshape(dp_count, rows, summed.shape[1])

    mlp_arrived = deal(after(mlp_sums, out_rows), "chip")
    d_query, d_pair_own, *d_pairs = attend_back(
        project, after(d_attended, out_rows, summed_gate), pairs, logs, bias, cosine, sine
    )
    summed_up = over_sp(after(up_total, summed_gate))
    pair_arrived = [shift(sent, sp_count, -1 - j) for j, sent in enumerate(d_pairs)]
    out_total = row_grad(after(out_rows, d_query), [attended_own, attended_other], core_only, chips)
    d_pair = pair_back(after(d_pair_own, out_total), pair_arrived, cosine, sine)
    summed_out = over_sp(after(out_total, summed_up, d_pair))
    tile_of = [m * KEY_VALUE_HEADS // dp_count for m in members]
    mlp_out = jnp.sum(mlp_arrived.reshape(chips, shard, width).astype(F32), axis=0)
    output = (resid + mlp_out).astype(BF16)
    project_blocks = windows(
        [d_query, d_pair],
        [[m * query_local, t * LANES] for m, t in zip(members, tile_of)],
        [query_local, LANES],
        [mlp_arrived],
    )
    project_columns = deal(project_blocks, MEMBERS)
    grad_output_proj = summed_out.astype(F32)
    project_total, project_done = dealt_grad(
        [normed_own, normed_other], after(project_columns, summed_out), width, sp_count, dp_count, core_only
    )
    summed_project = over_sp(after(project_total, summed_out))
    d_project = after(jnp.concatenate([d_query, d_pair], axis=1), project_done)
    (input_grad,) = member_product(
        False, chips, d_project, in_own, in_other, core_only, [d_resid, inputs[0], gain_one],
        [jax.ShapeDtypeStruct((shard, width), BF16)], finish_input_grad, "input_grad",
    )
    summed_ff = jnp.concatenate([summed_gate, summed_up, summed_down], axis=1)
    back_ff = to_owner(after(summed_ff, project_done))
    back_gate, back_up, back_down = (back_ff[:, :, i * ff_local : (i + 1) * ff_local] for i in range(3))

    def ff_columns(back):
        parts = []
        for m in members:
            start = (first[m] - begin[m]) * LANES
            parts.append(back[m][:, start : start + (first[m + 1] - first[m]) * LANES])
        return jnp.concatenate(parts, axis=1).astype(F32)

    grad_down, grad_gate, grad_up = (ff_columns(b) for b in (back_down, back_gate, back_up))
    back = to_owner(after(summed_project, back_ff)).astype(F32)
    grad_query = jnp.concatenate([back[m][:, :query_local] for m in members], axis=1)
    pair_grads = [back[h * dp_count // KEY_VALUE_HEADS][:, query_local:] for h in heads]
    grad_key = jnp.concatenate([g[:, :HEAD_SIZE] for g in pair_grads], axis=1)
    grad_value = jnp.concatenate([g[:, HEAD_SIZE:] for g in pair_grads], axis=1)
    grad_attn_gain = (
        jnp.sum(w_query.astype(F32) * grad_query, axis=1)
        + jnp.sum(key_weight.astype(F32) * grad_key, axis=1)
        + jnp.sum(value_weight.astype(F32) * grad_value, axis=1)
    ) / attn_gain.astype(F32)
    grad_mlp_gain = (
        jnp.sum(w_gate.astype(F32) * grad_gate, axis=1) + jnp.sum(w_up.astype(F32) * grad_up, axis=1)
    ) / mlp_gain.astype(F32)
    return (
        output[None],
        input_grad[None],
        grad_attn_gain,
        grad_query,
        grad_key,
        grad_value,
        grad_output_proj,
        grad_mlp_gain,
        grad_gate,
        grad_up,
        grad_down,
    )


def solution(mesh):
    shape = (mesh.shape["dp"] // 2, 2, mesh.shape["sp"])
    cores = Mesh(mesh.devices.reshape(shape), EVERY)
    token_spec = P(MEMBERS, "sp", None)
    vector_spec = P(EVERY)
    weight_spec = P(EVERY, None)
    return jax.shard_map(
        local,
        mesh=cores,
        in_specs=(
            token_spec,
            token_spec,
            P(MEMBERS, None),
            vector_spec,
            weight_spec,
            weight_spec,
            weight_spec,
            weight_spec,
            vector_spec,
            weight_spec,
            weight_spec,
            weight_spec,
        ),
        out_specs=(
            token_spec,
            token_spec,
            vector_spec,
            weight_spec,
            weight_spec,
            weight_spec,
            weight_spec,
            vector_spec,
            weight_spec,
            weight_spec,
            weight_spec,
        ),
        check_vma=False,
    )
```

```python
import math

import jax
import jax.numpy as jnp
from jax import lax
from jax.experimental import pallas as pl
from jax.experimental.pallas import tpu as pltpu
from jax.sharding import Mesh, PartitionSpec as P

HQ = 32
KEY_VALUE_HEADS = 4
HEAD_SIZE = 64
UNIT = 128
DOC_UNITS = 8
LANES = 128
GROUP = HQ // KEY_VALUE_HEADS
QUERY_WIDTH = HQ * HEAD_SIZE
KEY_WIDTH = KEY_VALUE_HEADS * HEAD_SIZE
PROJECT = QUERY_WIDTH + 2 * KEY_WIDTH
BLOCK = GROUP * HEAD_SIZE

EPSILON = 1e-05
MASKED = -1e30
SCALE = HEAD_SIZE ** (-0.5)
F32 = jnp.float32
BF16 = jnp.bfloat16
MEMBERS = ("chip", "core")
EVERY = ("chip", "core", "sp")
VMEM_LIMIT = 48 * 1024 * 1024
NO_COST = pl.CostEstimate(flops=0, bytes_accessed=0, transcendentals=0)


def cost(flops):
    return pl.CostEstimate(flops=int(flops), bytes_accessed=0, transcendentals=0)


def doc_layout(unit_lengths, places):
    token_lengths = unit_lengths * UNIT
    ends = jnp.cumsum(token_lengths)
    passed = places[:, None] >= ends[None, :]
    return jnp.sum(jnp.where(passed, token_lengths[None, :], 0), axis=1)


def rope_tables(positions):
    half_dim = HEAD_SIZE // 2
    inverse = jnp.power(10000.0, jnp.arange(half_dim, dtype=F32) * (-2.0 / HEAD_SIZE))
    angles = positions.astype(F32)[:, None] * inverse[None, :]
    return jnp.tile(jnp.cos(angles), (1, 4)), jnp.tile(jnp.sin(angles), (1, 4))


def key_pieces(length, shard, docs):
    units, per = length // UNIT, shard // UNIT
    longest = min(DOC_UNITS, units - 2)
    needed = 1
    for unit in range(units):
        earliest = max(0, unit - longest + 1)
        if docs == 2 and unit >= longest:
            earliest = max(earliest, units - longest)
        needed = max(needed, unit // per - earliest // per + 1)
    return needed


def contract_last(left, right):
    return lax.dot_general(left, right, (((1,), (1,)), ((), ())), preferred_element_type=F32)


def contract_rows(left, right):
    return lax.dot_general(left, right, (((0,), (0,)), ((), ())), preferred_element_type=F32)


def first_half(shape):
    lane = lax.broadcasted_iota(jnp.int32, shape, 1)
    return lane % HEAD_SIZE < HEAD_SIZE // 2


def half_swap(values):
    half_dim, lanes = HEAD_SIZE // 2, values.shape[1]
    return jnp.where(
        first_half(values.shape),
        pltpu.roll(values, lanes - half_dim, 1),
        pltpu.roll(values, half_dim, 1),
    )


def member_product(by_rows, chips, values, own, other, core, extras, out_shapes, finish, name):
    tokens = values.shape[0]
    block, columns = own.shape[0] // chips, own.shape[1]
    width = columns if by_rows else 2 * own.shape[0]

    def kernel(core_ref, values_ref, own_ref, other_ref, *refs):
        extra_refs, out_refs, total_ref = refs[: len(extras)], refs[len(extras) : -1], refs[-1]
        chip, mine = pl.program_id(0), core_ref[0]
        places = [
            pl.ds(pl.multiple_of((chip * 2 + c) * block, LANES), block) for c in (mine, 1 - mine)
        ]
        if by_rows:
            part = jnp.dot(values_ref[:, places[0]], own_ref[...], preferred_element_type=F32)
            part = part + jnp.dot(values_ref[:, places[1]], other_ref[...], preferred_element_type=F32)

            @pl.when(chip == 0)
            def _():
                total_ref[...] = part

            @pl.when(chip > 0)
            def _():
                total_ref[...] += part
        else:
            used = values_ref.shape[1]
            total_ref[:, places[0]] = contract_last(values_ref[...], own_ref[:, :used])
            total_ref[:, places[1]] = contract_last(values_ref[...], other_ref[:, :used])

        @pl.when(chip == chips - 1)
        def _():
            finish(total_ref, extra_refs, out_refs)

    def whole(shape):
        return pl.BlockSpec(shape, lambda i: (0,) * len(shape))

    return pl.pallas_call(
        kernel,
        grid=(chips,),
        in_specs=[
            pl.BlockSpec(memory_space=pltpu.SMEM),
            whole(values.shape),
            pl.BlockSpec((block, columns), lambda i: (i, 0)),
            pl.BlockSpec((block, columns), lambda i: (i, 0)),
        ]
        + [whole(e.shape) for e in extras],
        out_specs=[whole(o.shape) for o in out_shapes],
        out_shape=out_shapes,
        scratch_shapes=[pltpu.VMEM((tokens, width), F32)],
        compiler_params=pltpu.CompilerParams(vmem_limit_bytes=VMEM_LIMIT),
        cost_estimate=NO_COST,
        name=name,
    )(core, values, own, other, *extras)


def project_kernel(
    core_ref, scaled_ref, own_ref, other_ref, cos_ref, sin_ref, out_ref, normed_ref, gains_ref, total_ref
):
    chip, mine = pl.program_id(0), core_ref[0]
    block = own_ref.shape[0]
    part = None
    for ref, c in ((own_ref, mine), (other_ref, 1 - mine)):
        place = pl.ds(pl.multiple_of((chip * 2 + c) * block, LANES), block)
        gains = ref[:, PROJECT : PROJECT + LANES].astype(F32).T[:8]
        gains_ref[:, place] = gains
        normed = (scaled_ref[:, place] * gains[:1]).astype(BF16)
        normed_ref[:, place] = normed
        term = jnp.dot(normed, ref[:, :PROJECT], preferred_element_type=F32)
        part = term if part is None else part + term

    @pl.when(chip == 0)
    def _():
        total_ref[...] = part

    @pl.when(chip > 0)
    def _():
        total_ref[...] += part

    @pl.when(chip == pl.num_programs(0) - 1)
    def _():
        cosine = jnp.concatenate([cos_ref[...]] * (BLOCK // LANES), axis=1)
        sine = jnp.concatenate([sin_ref[...]] * (BLOCK // LANES), axis=1)
        for step in range(PROJECT // BLOCK):
            where = slice(step * BLOCK, (step + 1) * BLOCK)
            values = total_ref[:, where]
            swapped = half_swap(values)
            turned = values * cosine + jnp.where(first_half(values.shape), -swapped, swapped) * sine
            if step < QUERY_WIDTH // BLOCK:
                result = turned * SCALE
            else:
                lane = lax.broadcasted_iota(jnp.int32, values.shape, 1)
                result = jnp.where(lane % LANES < HEAD_SIZE, turned, values)
            out_ref[:, where] = result.astype(BF16)


def projections(chips, scaled, own, other, core, cosine, sine):
    tokens, width = scaled.shape
    block, columns = own.shape[0] // chips, own.shape[1]

    def whole(shape):
        return pl.BlockSpec(shape, lambda i: (0, 0))

    return pl.pallas_call(
        project_kernel,
        grid=(chips,),
        in_specs=[
            pl.BlockSpec(memory_space=pltpu.SMEM),
            whole((tokens, width)),
            pl.BlockSpec((block, columns), lambda i: (i, 0)),
            pl.BlockSpec((block, columns), lambda i: (i, 0)),
            whole((tokens, LANES)),
            whole((tokens, LANES)),
        ],
        out_specs=[whole((tokens, PROJECT)), whole((tokens, width)), whole((8, width))],
        out_shape=[
            jax.ShapeDtypeStruct((tokens, PROJECT), BF16),
            jax.ShapeDtypeStruct((tokens, width), BF16),
            jax.ShapeDtypeStruct((8, width), F32),
        ],
        scratch_shapes=[pltpu.VMEM((tokens, PROJECT), F32)],
        compiler_params=pltpu.CompilerParams(vmem_limit_bytes=VMEM_LIMIT),
        cost_estimate=NO_COST,
        name="project",
    )(core, scaled, own, other, cosine, sine)


def finish_residual(total_ref, extras, outs):
    tokens_ref, gain_ref = extras
    resid = tokens_ref[...].astype(F32) + total_ref[...]
    inverse = lax.rsqrt(jnp.mean(resid * resid, axis=1, keepdims=True) + EPSILON)
    outs[0][...] = resid
    outs[1][...] = (resid * inverse * gain_ref[...]).astype(BF16)


def finish_cast(total_ref, extras, outs):
    outs[0][...] = total_ref[...].astype(BF16)


def finish_input_grad(total_ref, extras, outs):
    d_resid_ref, tokens_ref, gain_ref = extras
    tokens = tokens_ref[...].astype(F32)
    inverse = lax.rsqrt(jnp.mean(tokens * tokens, axis=1, keepdims=True) + EPSILON)
    mixed = total_ref[...] * gain_ref[...]
    along = jnp.mean(mixed * tokens, axis=1, keepdims=True)
    grad = d_resid_ref[...] + inverse * mixed - tokens * (inverse * inverse * inverse) * along
    outs[0][...] = grad.astype(BF16)


def attend_kernel(query_ref, pair_ref, bias_ref, out_ref, log_ref):
    key, value = pair_ref[:, :HEAD_SIZE], pair_ref[:, HEAD_SIZE:]
    for two in range(GROUP // 2):
        parts = []
        for head in (2 * two, 2 * two + 1):
            query = query_ref[:, head * HEAD_SIZE : (head + 1) * HEAD_SIZE]
            scores = contract_last(key, query) + bias_ref[...]
            largest = jnp.max(scores, axis=0, keepdims=True)
            weights = jnp.exp(scores - largest)
            totals = jnp.sum(weights, axis=0, keepdims=True)
            parts.append(contract_rows(value, weights.astype(BF16)) / totals)
            log_ref[head : head + 1, :] = largest + jnp.log(totals)
        both = jnp.concatenate(parts, axis=0)
        out_ref[:, two * LANES : (two + 1) * LANES] = both.T.astype(BF16)


def attend(project, pairs, bias):
    tokens, keys = project.shape[0], pairs.shape[0]
    return pl.pallas_call(
        attend_kernel,
        grid=(KEY_VALUE_HEADS,),
        in_specs=[
            pl.BlockSpec((tokens, BLOCK), lambda i: (0, i)),
            pl.BlockSpec((keys, LANES), lambda i: (0, i)),
            pl.BlockSpec((keys, tokens), lambda i: (0, 0)),
        ],
        out_specs=[
            pl.BlockSpec((tokens, BLOCK), lambda i: (0, i)),
            pl.BlockSpec((GROUP, tokens), lambda i: (i, 0)),
        ],
        out_shape=[
            jax.ShapeDtypeStruct((tokens, QUERY_WIDTH), BF16),
            jax.ShapeDtypeStruct((HQ, tokens), F32),
        ],
        compiler_params=pltpu.CompilerParams(vmem_limit_bytes=VMEM_LIMIT),
        cost_estimate=NO_COST,
        name="attend",
    )(project, pairs, bias)


def attend_back_kernel(
    query_ref, grad_ref, pair_ref, log_ref, bias_ref, cos_ref, sin_ref, d_query_ref, *d_pair_refs
):
    key, value = pair_ref[:, :HEAD_SIZE], pair_ref[:, HEAD_SIZE:]
    d_key = jnp.zeros((key.shape[0], HEAD_SIZE), F32)
    d_value = jnp.zeros((key.shape[0], HEAD_SIZE), F32)
    for two in range(GROUP // 2):
        parts = []
        for head in (2 * two, 2 * two + 1):
            query = query_ref[:, head * HEAD_SIZE : (head + 1) * HEAD_SIZE]
            grad = grad_ref[:, head * HEAD_SIZE : (head + 1) * HEAD_SIZE]
            scores = contract_last(key, query) + bias_ref[...]
            probs = jnp.exp(scores - log_ref[head : head + 1, :])
            d_probs = contract_last(value, grad)
            row_dot = jnp.sum(probs * d_probs, axis=0, keepdims=True)
            d_scores = (probs * (d_probs - row_dot)).astype(BF16)
            d_value = d_value + jnp.dot(probs.astype(BF16), grad, preferred_element_type=F32)
            d_key = d_key + jnp.dot(d_scores, query, preferred_element_type=F32)
            parts.append(contract_rows(key, d_scores) * SCALE)
        both = jnp.concatenate(parts, axis=0).T.astype(BF16).astype(F32)
        swapped = half_swap(both * sin_ref[...])
        back = both * cos_ref[...] + jnp.where(first_half(both.shape), swapped, -swapped)
        d_query_ref[:, two * LANES : (two + 1) * LANES] = back.astype(BF16)
    d_pair = jnp.concatenate([d_key, d_value], axis=1)
    shard = query_ref.shape[0]
    for piece, ref in enumerate(d_pair_refs):
        ref[...] = d_pair[piece * shard : (piece + 1) * shard].astype(ref.dtype)


def attend_back(project, grads, pairs, logs, bias, cosine, sine):
    tokens, keys = project.shape[0], pairs.shape[0]
    return pl.pallas_call(
        attend_back_kernel,
        grid=(KEY_VALUE_HEADS,),
        in_specs=[
            pl.BlockSpec((tokens, BLOCK), lambda i: (0, i)),
            pl.BlockSpec((tokens, BLOCK), lambda i: (0, i)),
            pl.BlockSpec((keys, LANES), lambda i: (0, i)),
            pl.BlockSpec((GROUP, tokens), lambda i: (i, 0)),
            pl.BlockSpec((keys, tokens), lambda i: (0, 0)),
            pl.BlockSpec((tokens, LANES), lambda i: (0, 0)),
            pl.BlockSpec((tokens, LANES), lambda i: (0, 0)),
        ],
        out_specs=[
            pl.BlockSpec((tokens, BLOCK), lambda i: (0, i)),
        ]
        + [pl.BlockSpec((tokens, LANES), lambda i: (0, i))] * (keys // tokens),
        out_shape=[
            jax.ShapeDtypeStruct((tokens, QUERY_WIDTH), BF16),
            jax.ShapeDtypeStruct((tokens, 2 * KEY_WIDTH), F32),
        ]
        + [jax.ShapeDtypeStruct((tokens, 2 * KEY_WIDTH), BF16)] * (keys // tokens - 1),
        compiler_params=pltpu.CompilerParams(vmem_limit_bytes=VMEM_LIMIT),
        cost_estimate=cost(64 * HQ * tokens * keys * HEAD_SIZE),
        name="attend_back",
    )(project, grads, pairs, logs, bias, cosine, sine)


def load_rows(sources, held, sems):
    copies = []
    for (ref, first), to in zip(sources, held):
        for j in range(ref.shape[0]):
            part = ref.at[j, :, :, pl.ds(first, to.shape[3])]
            copies.append(pltpu.make_async_copy(part, to.at[:, j], sems.at[len(copies)]))
            copies[-1].start()
    for copy in copies:
        copy.wait()


def as_rows(ref):
    return ref[...].reshape(-1, ref.shape[3])


def feed_forward(normed, grads, weight, local):
    tokens, width = normed.shape
    sp_count, dp_count, rows, columns = weight.shape
    block = min(tokens, 256)
    both, last = lanes_of(2 * local), lanes_of(local)

    def kernel(normed_ref, grad_ref, weight_ref, hidden_ref, d_both_ref, held, sems):
        @pl.when(pl.program_id(0) == 0)
        def _():
            load_rows([(weight_ref, 0)], [held], sems)

        weights = held[...].reshape(width, columns)
        pair = jnp.dot(normed_ref[...], weights[:, :both], preferred_element_type=F32)
        d_hidden = jnp.dot(grad_ref[...], weights[:, both:], preferred_element_type=F32)
        gate, up = pair[:, :last], moved(pair, -local)[:, :last]
        sigmoid_gate = jax.nn.sigmoid(gate)
        activated = gate * sigmoid_gate
        hidden_ref[...] = first_lanes(activated * up, local).astype(BF16)
        d_gate = first_lanes(d_hidden * up * (sigmoid_gate * (1.0 + gate * (1.0 - sigmoid_gate))), local)
        d_up = first_lanes(d_hidden * activated, local)
        d_both_ref[...] = (widened(d_gate, both) + moved(widened(d_up, both), local)).astype(BF16)

    return pl.pallas_call(
        kernel,
        grid=(tokens // block,),
        in_specs=[
            pl.BlockSpec((block, width), lambda i: (i, 0)),
            pl.BlockSpec((block, width), lambda i: (i, 0)),
            pl.BlockSpec(memory_space=pl.ANY),
        ],
        out_specs=[
            pl.BlockSpec((block, last), lambda i: (i, 0)),
            pl.BlockSpec((block, both), lambda i: (i, 0)),
        ],
        out_shape=[
            jax.ShapeDtypeStruct((tokens, last), BF16),
            jax.ShapeDtypeStruct((tokens, both), BF16),
        ],
        scratch_shapes=[
            pltpu.VMEM((dp_count, sp_count, rows, columns), BF16),
            pltpu.SemaphoreType.DMA((sp_count,)),
        ],
        compiler_params=pltpu.CompilerParams(vmem_limit_bytes=VMEM_LIMIT),
        cost_estimate=NO_COST,
        name="feed_forward",
    )(normed, grads, weight)


def times_weights(values, weights):
    terms = len(values)
    count, columns = values[0].shape
    sp_count, dp_count, rows, _ = weights[0][0].shape
    width = sp_count * dp_count * rows
    block = min(count, 256)

    def kernel(*refs):
        value_refs, weight_refs = refs[:terms], refs[terms : 2 * terms]
        out_ref, held, sems = refs[2 * terms], refs[2 * terms + 1 : -1], refs[-1]

        @pl.when(pl.program_id(0) == 0)
        def _():
            load_rows([(r, w[1]) for r, w in zip(weight_refs, weights)], held, sems)

        total = contract_last(value_refs[0][...], as_rows(held[0]))
        for ref, weight in zip(value_refs[1:], held[1:]):
            total = total + contract_last(ref[...], as_rows(weight))
        out_ref[...] = total.astype(BF16)

    return pl.pallas_call(
        kernel,
        grid=(count // block,),
        in_specs=[pl.BlockSpec((block, columns), lambda i: (i, 0))] * terms
        + [pl.BlockSpec(memory_space=pl.ANY)] * terms,
        out_specs=pl.BlockSpec((block, width), lambda i: (i, 0)),
        out_shape=jax.ShapeDtypeStruct((count, width), BF16),
        scratch_shapes=[pltpu.VMEM((dp_count, sp_count, rows, columns), BF16)] * terms
        + [pltpu.SemaphoreType.DMA((terms * sp_count,))],
        compiler_params=pltpu.CompilerParams(vmem_limit_bytes=VMEM_LIMIT),
        cost_estimate=NO_COST,
        name="times_weights",
    )(*values, *(w[0] for w in weights))


def row_grad(dealt, rights, core, chips):
    tokens, columns = rights[0].shape
    rows = dealt.shape[1]
    block = min(columns, 512)

    def kernel(core_ref, left_ref, left2_ref, right_ref, right2_ref, out_ref):
        total = contract_rows(left_ref[...].reshape(tokens, rows), right_ref[...])
        total = total + contract_rows(left2_ref[...].reshape(tokens, rows), right2_ref[...])
        out_ref[...] = total.astype(BF16)

    dealt = dealt.reshape(chips, 2, tokens // chips, rows)
    part = (chips, 1, tokens // chips, rows)
    return pl.pallas_call(
        kernel,
        grid_spec=pltpu.PrefetchScalarGridSpec(
            num_scalar_prefetch=1,
            grid=(columns // block,),
            in_specs=[
                pl.BlockSpec(part, lambda i, c: (0, c[0], 0, 0)),
                pl.BlockSpec(part, lambda i, c: (0, 1 - c[0], 0, 0)),
                pl.BlockSpec((tokens, block), lambda i, c: (0, i)),
                pl.BlockSpec((tokens, block), lambda i, c: (0, i)),
            ],
            out_specs=pl.BlockSpec((rows, block), lambda i, c: (0, i)),
        ),
        out_shape=jax.ShapeDtypeStruct((rows, columns), BF16),
        compiler_params=pltpu.CompilerParams(vmem_limit_bytes=VMEM_LIMIT),
        cost_estimate=NO_COST,
        name="row_grad",
    )(core, dealt, dealt, *rights)


def dealt_grad(lefts, dealt, width, sp_count, dp_count, core):
    tokens = lefts[0].shape[0]
    columns = dealt.shape[1]
    block = width // dp_count
    rows = block // sp_count
    chips = dp_count // 2

    def kernel(core_ref, left_ref, left2_ref, right_ref, right2_ref, out_ref, done_ref):
        total = contract_rows(left_ref[...], right_ref[...].reshape(tokens, columns))
        total = total + contract_rows(left2_ref[...], right2_ref[...].reshape(tokens, columns))
        out_ref[...] = total.astype(BF16).reshape(sp_count, 1, rows, columns)
        done_ref[...] = jnp.zeros_like(done_ref)

    dealt = dealt.reshape(chips, 2, tokens // chips, columns)
    part = (chips, 1, tokens // chips, columns)
    total, done = pl.pallas_call(
        kernel,
        grid_spec=pltpu.PrefetchScalarGridSpec(
            num_scalar_prefetch=1,
            grid=(dp_count,),
            in_specs=[
                pl.BlockSpec((tokens, block), lambda i, c: (0, i)),
                pl.BlockSpec((tokens, block), lambda i, c: (0, i)),
                pl.BlockSpec(part, lambda i, c: (0, c[0], 0, 0)),
                pl.BlockSpec(part, lambda i, c: (0, 1 - c[0], 0, 0)),
            ],
            out_specs=[
                pl.BlockSpec((sp_count, 1, rows, columns), lambda i, c: (0, i, 0, 0)),
                pl.BlockSpec((8, LANES), lambda i, c: (0, 0)),
            ],
        ),
        out_shape=[
            jax.ShapeDtypeStruct((sp_count, dp_count, rows, columns), BF16),
            jax.ShapeDtypeStruct((8, LANES), F32),
        ],
        compiler_params=pltpu.CompilerParams(vmem_limit_bytes=VMEM_LIMIT),
        cost_estimate=NO_COST,
        name="dealt_grad",
    )(core, *lefts, dealt, dealt)
    return total.reshape(width, columns), done


def weight_grad(lefts, rights, width, sp_count, dp_count):
    tokens = lefts[0].shape[0]
    columns = rights[0].shape[1]
    block = width // dp_count
    rows = block // sp_count

    def kernel(left_ref, left2_ref, right_ref, right2_ref, out_ref, done_ref):
        total = contract_rows(left_ref[...], right_ref[...])
        total = total + contract_rows(left2_ref[...], right2_ref[...])
        out_ref[...] = total.astype(BF16).reshape(sp_count, 1, rows, columns)
        done_ref[...] = jnp.zeros_like(done_ref)

    total, done = pl.pallas_call(
        kernel,
        grid=(dp_count,),
        in_specs=[pl.BlockSpec((tokens, block), lambda i: (0, i))] * 2
        + [pl.BlockSpec((tokens, columns), lambda i: (0, 0))] * 2,
        out_specs=[
            pl.BlockSpec((sp_count, 1, rows, columns), lambda i: (0, i, 0, 0)),
            pl.BlockSpec((8, LANES), lambda i: (0, 0)),
        ],
        out_shape=[
            jax.ShapeDtypeStruct((sp_count, dp_count, rows, columns), BF16),
            jax.ShapeDtypeStruct((8, LANES), F32),
        ],
        compiler_params=pltpu.CompilerParams(vmem_limit_bytes=VMEM_LIMIT),
        cost_estimate=NO_COST,
        name="weight_grad",
    )(*lefts, *rights)
    return total.reshape(width, columns), done


def assemble(pieces, starts, first=0, columns=None, deps=()):
    count = len(pieces)
    total = sum(piece.shape[0] for piece in pieces)
    columns = columns or pieces[0].shape[1]

    def kernel(starts_ref, *refs):
        out_ref, held, in_sems, out_sems = refs[count + len(deps) :]
        inward, outward = [], []
        for i in range(count):
            place = pl.ds(pl.multiple_of(starts_ref[i], 32), pieces[i].shape[0])
            piece = refs[i].at[:, pl.ds(first, columns)]
            inward.append(pltpu.make_async_copy(piece, held.at[place, :], in_sems.at[i]))
            outward.append(
                pltpu.make_async_copy(held.at[place, :], out_ref.at[place, :], out_sems.at[i])
            )
            inward[-1].start()
        for i in range(count):
            inward[i].wait()
            outward[i].start()
        for copy in outward:
            copy.wait()

    return pl.pallas_call(
        kernel,
        in_specs=[pl.BlockSpec(memory_space=pltpu.SMEM)]
        + [pl.BlockSpec(memory_space=pl.ANY)] * (count + len(deps)),
        out_specs=pl.BlockSpec(memory_space=pl.ANY),
        out_shape=jax.ShapeDtypeStruct((total, columns), pieces[0].dtype),
        scratch_shapes=[
            pltpu.VMEM((total, columns), pieces[0].dtype),
            pltpu.SemaphoreType.DMA((count,)),
            pltpu.SemaphoreType.DMA((count,)),
        ],
        compiler_params=pltpu.CompilerParams(vmem_limit_bytes=VMEM_LIMIT),
        cost_estimate=NO_COST,
        name="assemble",
    )(jnp.stack([jnp.asarray(s, jnp.int32) for s in starts]), *pieces, *deps)


def windows(arrays, starts, sizes, deps=()):
    count, rows, total = len(starts), arrays[0].shape[0], sum(sizes)

    def kernel(*refs):
        out_ref = refs[-1]
        for k in range(count):
            at = 0
            for i, size in enumerate(sizes):
                out_ref[k * rows : (k + 1) * rows, at : at + size] = refs[i][:, starts[k][i] : starts[k][i] + size]
                at += size

    return pl.pallas_call(
        kernel,
        in_specs=[pl.BlockSpec(memory_space=pltpu.VMEM)] * len(arrays)
        + [pl.BlockSpec(memory_space=pl.ANY)] * len(deps),
        out_specs=pl.BlockSpec(memory_space=pltpu.VMEM),
        out_shape=jax.ShapeDtypeStruct((count * rows, total), arrays[0].dtype),
        compiler_params=pltpu.CompilerParams(vmem_limit_bytes=VMEM_LIMIT),
        cost_estimate=NO_COST,
        name="windows",
    )(*arrays, *deps)


def summed(left, right):
    rows, columns = left.shape
    block = min(rows, 256)

    def kernel(left_ref, right_ref, out_ref):
        out_ref[...] = (left_ref[...].astype(F32) + right_ref[...].astype(F32)).astype(BF16)

    spec = pl.BlockSpec((block, columns), lambda i: (i, 0))
    return pl.pallas_call(
        kernel,
        grid=(rows // block,),
        in_specs=[spec] * 2,
        out_specs=spec,
        out_shape=jax.ShapeDtypeStruct(left.shape, BF16),
        cost_estimate=NO_COST,
        compiler_params=pltpu.CompilerParams(vmem_limit_bytes=VMEM_LIMIT),
        name="summed",
    )(left, right)


def residual_grad(arrived, grads, resid, gain):
    chips, tokens, width = arrived.shape
    block = min(tokens, 64)

    def kernel(arrived_ref, grad_ref, resid_ref, gain_ref, d_resid_ref, rounded_ref):
        total = arrived_ref[0].astype(F32)
        for i in range(1, chips):
            total = total + arrived_ref[i].astype(F32)
        resid = resid_ref[...]
        inverse = lax.rsqrt(jnp.mean(resid * resid, axis=1, keepdims=True) + EPSILON)
        mixed = total * gain_ref[...]
        along = jnp.mean(mixed * resid, axis=1, keepdims=True)
        d_resid = grad_ref[...].astype(F32) + inverse * mixed - resid * (inverse * inverse * inverse) * along
        d_resid_ref[...] = d_resid
        rounded_ref[...] = d_resid.astype(BF16)

    spec = pl.BlockSpec((block, width), lambda i: (i, 0))
    return pl.pallas_call(
        kernel,
        grid=(tokens // block,),
        in_specs=[
            pl.BlockSpec((chips, block, width), lambda i: (0, i, 0)),
            spec,
            spec,
            pl.BlockSpec((1, width), lambda i: (0, 0)),
        ],
        out_specs=[spec, spec],
        out_shape=[jax.ShapeDtypeStruct((tokens, width), F32), jax.ShapeDtypeStruct((tokens, width), BF16)],
        compiler_params=pltpu.CompilerParams(vmem_limit_bytes=VMEM_LIMIT),
        cost_estimate=NO_COST,
        name="residual_grad",
    )(arrived, grads, resid, gain)


def pair_back(own, arrived, cosine, sine):
    tokens, columns = own.shape
    count = len(arrived)

    def kernel(own_ref, cos_ref, sin_ref, *refs):
        total = own_ref[...]
        for ref in refs[:count]:
            total = total + ref[...].astype(F32)
        total = total.astype(BF16).astype(F32)
        times = columns // LANES
        cosine = jnp.concatenate([cos_ref[...]] * times, axis=1)
        sine = jnp.concatenate([sin_ref[...]] * times, axis=1)
        swapped = half_swap(total * sine)
        back = total * cosine + jnp.where(first_half(total.shape), swapped, -swapped)
        lane = lax.broadcasted_iota(jnp.int32, total.shape, 1)
        refs[count][...] = jnp.where(lane % LANES < HEAD_SIZE, back, total).astype(BF16)

    return pl.pallas_call(
        kernel,
        out_shape=jax.ShapeDtypeStruct((tokens, columns), BF16),
        compiler_params=pltpu.CompilerParams(vmem_limit_bytes=VMEM_LIMIT),
        cost_estimate=NO_COST,
        name="pair_back",
    )(own, cosine, sine, *arrived)


def lanes_of(count):
    return -(-count // LANES) * LANES


def moved(values, by):
    return values if by % values.shape[1] == 0 else pltpu.roll(values, by % values.shape[1], 1)


def first_lanes(values, count):
    lane = lax.broadcasted_iota(jnp.int32, values.shape, 1)
    return jnp.where(lane < count, values, 0.0)


def widened(values, lanes):
    if values.shape[1] >= lanes:
        return values[:, :lanes]
    return jnp.concatenate([values, jnp.zeros((values.shape[0], lanes - values.shape[1]), values.dtype)], axis=1)


def pack_columns(gate, up, down, dp_count):
    rows, ff = gate.shape
    local = ff // dp_count
    together = LANES // math.gcd(local, LANES)
    group = together * local
    both, last = lanes_of(2 * local), lanes_of(local)

    def kernel(gate_ref, up_ref, down_ref, out_ref):
        for m in range(dp_count):
            place = slice(m // together * group, m // together * group + group)
            parts = [
                first_lanes(moved(ref[:, place].astype(F32), -(m % together) * local), local)
                for ref in (gate_ref, up_ref, down_ref)
            ]
            pair = widened(parts[0], both) + moved(widened(parts[1], both), local)
            out_ref[m * rows : (m + 1) * rows, :both] = pair.astype(BF16)
            out_ref[m * rows : (m + 1) * rows, both:] = widened(parts[2], last).astype(BF16)

    return pl.pallas_call(
        kernel,
        out_shape=jax.ShapeDtypeStruct((dp_count * rows, both + last), BF16),
        compiler_params=pltpu.CompilerParams(vmem_limit_bytes=VMEM_LIMIT),
        cost_estimate=NO_COST,
        name="pack_columns",
    )(gate, up, down)


def unpack_columns(packed, ff):
    dp_count, rows, _ = packed.shape
    local = ff // dp_count
    together = LANES // math.gcd(local, LANES)
    group = together * local
    both = lanes_of(2 * local)

    def kernel(packed_ref, *outs):
        for first in range(0, dp_count, together):
            sums = [jnp.zeros((rows, group), F32) for _ in outs]
            for i in range(together):
                block = packed_ref[first + i].astype(F32)
                pair, last = block[:, :both], block[:, both:]
                for k, part in enumerate((pair, moved(pair, -local), last)):
                    sums[k] = sums[k] + moved(widened(first_lanes(part, local), group), i * local)
            place = slice(first * local, first * local + group)
            for out, total in zip(outs, sums):
                out[:, place] = total

    return pl.pallas_call(
        kernel,
        out_shape=[jax.ShapeDtypeStruct((rows, ff), F32)] * 3,
        compiler_params=pltpu.CompilerParams(vmem_limit_bytes=VMEM_LIMIT),
        cost_estimate=NO_COST,
        name="unpack_columns",
    )(packed)


def after(value, *others):
    def kernel(*refs):
        del refs

    return pl.pallas_call(
        kernel,
        in_specs=[pl.BlockSpec(memory_space=pl.ANY)] * (1 + len(others)),
        out_specs=pl.BlockSpec(memory_space=pl.ANY),
        out_shape=jax.ShapeDtypeStruct(value.shape, value.dtype),
        input_output_aliases={0: 0},
        cost_estimate=NO_COST,
        name="after",
    )(value, *others)


def spread(value, axis, *others):
    count, rows = lax.axis_size(axis), value.shape[0]
    copies = jnp.broadcast_to(value[None], (count,) + value.shape).reshape(count * rows, -1)
    if others:
        copies = after(copies, *others)
    return lax.all_to_all(copies, axis, split_axis=0, concat_axis=0, tiled=True)


def sp_rows(value, sp_count, sp_index):
    rows = value.shape[0]
    pieces, starts = [value], [sp_index * rows]
    for j in range(1, sp_count):
        pieces.append(lax.ppermute(value, "sp", [(i, (i + j) % sp_count) for i in range(sp_count)]))
        starts.append((sp_index - j) % sp_count * rows)
    return assemble(pieces, starts)


def swap_cores(value):
    return lax.ppermute(value, "core", [(0, 1), (1, 0)])


def deal(value, axis):
    return lax.all_to_all(value, axis, split_axis=0, concat_axis=0, tiled=True)


def shift(value, count, by):
    pairs = [(i, i + by) for i in range(count) if 0 <= i + by < count]
    return lax.ppermute(value, "sp", pairs)


def local(
    inputs,
    cotangent,
    unit_lengths,
    attn_gain,
    w_query,
    key_weight,
    value_weight,
    w_output,
    mlp_gain,
    w_gate,
    w_up,
    w_down,
):
    chips = lax.axis_size("chip")
    dp_count = 2 * chips
    sp_count = lax.axis_size("sp")
    core = lax.axis_index("core")
    member = lax.axis_index("chip") * 2 + core
    core_only = core.astype(jnp.int32)[None]
    sp_index = lax.axis_index("sp")
    shard = inputs.shape[1]
    width = inputs.shape[2]
    length = shard * sp_count
    rows = w_query.shape[0]
    ff = w_gate.shape[1]
    query_local = QUERY_WIDTH // dp_count
    heads = range(KEY_VALUE_HEADS)
    members = range(dp_count)

    def head_columns(array, head):
        return array[:, head * HEAD_SIZE : (head + 1) * HEAD_SIZE]

    ff_local = ff // dp_count
    both_lanes = lanes_of(2 * ff_local)

    pair_columns = [head_columns(w, h) for h in heads for w in (key_weight, value_weight)]
    gains_local = jnp.pad(jnp.stack([attn_gain, mlp_gain], axis=1), ((0, 0), (0, LANES - 2)))
    in_local = jnp.concatenate([w_query] + pair_columns + [gains_local], axis=1)
    in_group = sp_rows(in_local, sp_count, sp_index)
    ff_mine = deal(pack_columns(w_gate, w_up, w_down, dp_count), MEMBERS)

    def along_sp(mine):
        return lax.all_gather(mine, "sp", axis=0).reshape(sp_count, dp_count, rows, mine.shape[1])

    out_group = sp_rows(w_output, sp_count, sp_index)
    ff_weight = along_sp(after(ff_mine, in_group))
    pair_weight, down_weight = (ff_weight, 0), (ff_weight, both_lanes)
    in_own = after(spread(in_group, "chip", ff_mine), out_group)
    in_other = swap_cores(in_own)
    out_own = spread(out_group, "chip", in_own)
    places = sp_index * shard + jnp.arange(shard, dtype=jnp.int32)
    begins = doc_layout(unit_lengths[0], places)
    cosine, sine = rope_tables(places - begins)
    pieces = key_pieces(length, shard, unit_lengths.shape[1])
    key_places = jnp.concatenate([places - j * shard for j in range(pieces)])[:, None]
    bias = jnp.where((key_places <= places[None]) & (key_places >= begins[None]), 0.0, MASKED)
    tokens_in = inputs[0].astype(F32)
    inv_one = lax.rsqrt(jnp.mean(tokens_in * tokens_in, axis=1, keepdims=True) + EPSILON)
    project, normed_one, gains = projections(
        chips, tokens_in * inv_one, in_own, in_other, core_only, cosine, sine
    )
    gain_one, gain_two = gains[:1], gains[1:2]
    pair = project[:, QUERY_WIDTH:]
    pairs = jnp.concatenate([pair] + [shift(pair, sp_count, j) for j in range(1, pieces)], axis=0)
    out_own = after(out_own, pairs)
    out_other = swap_cores(out_own)
    grad_own = spread(cotangent[0], "chip", out_own)
    grad_other = swap_cores(grad_own)
    attended, logs = attend(project, after(pairs, out_own), bias)
    resid, normed_two = member_product(
        False, chips, attended, out_own, out_other, core_only, [inputs[0], gain_two],
        [jax.ShapeDtypeStruct((shard, width), F32), jax.ShapeDtypeStruct((shard, width), BF16)],
        finish_residual, "out_project",
    )

    two_own = spread(normed_two, "chip", grad_own, ff_weight)
    two_other = swap_cores(two_own)
    normed_own = spread(normed_one, "chip", two_own)
    normed_other = swap_cores(normed_own)
    attended_own = spread(attended, "chip", normed_own)
    attended_other = swap_cores(attended_own)
    hidden_own, d_both_own = feed_forward(two_own, grad_own, ff_weight, ff_local)
    hidden_other, d_both_other = feed_forward(two_other, grad_other, ff_weight, ff_local)

    def for_sp(lefts, rights):
        return weight_grad(lefts, rights, width, sp_count, dp_count)

    def over_sp(total):
        return lax.psum_scatter(total, "sp", scatter_dimension=0, tiled=True)

    def chip_sums(own, other):
        return summed(own, swap_cores(other))

    down_total, down_done = for_sp([grad_own, grad_other], [hidden_own, hidden_other])
    summed_down = over_sp(down_total)
    d_both_other = after(d_both_other, down_total, normed_own)
    d_normed_other = times_weights([d_both_other], [pair_weight])
    d_both_own = after(d_both_own, d_normed_other)
    d_normed_own = times_weights([d_both_own], [pair_weight])
    d_normed_sums = after(chip_sums(d_normed_own, d_normed_other), attended_own)
    d_both_other = after(d_both_other, d_normed_sums)
    both_total, both_done = for_sp([two_own, two_other], [d_both_own, d_both_other])
    summed_both = over_sp(after(both_total, summed_down))
    mlp_other = times_weights([after(hidden_other, both_done)], [down_weight])
    mlp_own = times_weights([after(hidden_own, mlp_other)], [down_weight])
    mlp_sums = chip_sums(mlp_own, mlp_other)
    d_normed_two = after(deal(d_normed_sums, "chip"), mlp_sums).reshape(chips, shard, width)
    d_resid, d_attn_out = residual_grad(d_normed_two, cotangent[0], resid, gain_two)

    width_local = width // dp_count
    out_rows = deal(windows([d_attn_out], [[m * width_local] for m in members], [width_local]), MEMBERS)
    (d_attended,) = member_product(
        True, chips, d_attn_out, out_own, out_other, core_only, [],
        [jax.ShapeDtypeStruct((shard, QUERY_WIDTH), BF16)], finish_cast, "d_attended",
    )
    def to_owner(summed):
        return deal(summed, MEMBERS).reshape(dp_count, rows, summed.shape[1])

    mlp_arrived = deal(after(mlp_sums, out_rows), "chip")
    d_query, d_pair_own, *d_pairs = attend_back(
        project, after(d_attended, out_rows), pairs, logs, bias, cosine, sine
    )
    pair_arrived = [shift(sent, sp_count, -1 - j) for j, sent in enumerate(d_pairs)]
    out_total = row_grad(after(out_rows, d_query), [attended_own, attended_other], core_only, chips)
    d_pair = pair_back(after(d_pair_own, out_total), pair_arrived, cosine, sine)
    summed_out = over_sp(after(out_total, summed_both, d_pair))
    tile_of = [m * KEY_VALUE_HEADS // dp_count for m in members]
    mlp_out = jnp.sum(mlp_arrived.reshape(chips, shard, width).astype(F32), axis=0)
    output = (resid + mlp_out).astype(BF16)
    project_blocks = windows(
        [d_query, d_pair],
        [[m * query_local, t * LANES] for m, t in zip(members, tile_of)],
        [query_local, LANES],
        [mlp_arrived],
    )
    project_columns = deal(project_blocks, MEMBERS)
    grad_output_proj = summed_out.astype(F32)
    project_total, project_done = dealt_grad(
        [normed_own, normed_other], after(project_columns, summed_out), width, sp_count, dp_count, core_only
    )
    summed_project = over_sp(after(project_total, summed_out))
    d_project = after(jnp.concatenate([d_query, d_pair], axis=1), project_done)
    (input_grad,) = member_product(
        False, chips, d_project, in_own, in_other, core_only, [d_resid, inputs[0], gain_one],
        [jax.ShapeDtypeStruct((shard, width), BF16)], finish_input_grad, "input_grad",
    )
    summed_ff = jnp.concatenate([summed_both, summed_down], axis=1)
    back_ff = to_owner(after(summed_ff, project_done))
    grad_gate, grad_up, grad_down = unpack_columns(after(back_ff, summed_project), ff)
    back = to_owner(after(summed_project, back_ff)).astype(F32)
    grad_query = jnp.concatenate([back[m][:, :query_local] for m in members], axis=1)
    pair_grads = [back[h * dp_count // KEY_VALUE_HEADS][:, query_local:] for h in heads]
    grad_key = jnp.concatenate([g[:, :HEAD_SIZE] for g in pair_grads], axis=1)
    grad_value = jnp.concatenate([g[:, HEAD_SIZE:] for g in pair_grads], axis=1)
    grad_attn_gain = (
        jnp.sum(w_query.astype(F32) * grad_query, axis=1)
        + jnp.sum(key_weight.astype(F32) * grad_key, axis=1)
        + jnp.sum(value_weight.astype(F32) * grad_value, axis=1)
    ) / attn_gain.astype(F32)
    grad_mlp_gain = (
        jnp.sum(w_gate.astype(F32) * grad_gate, axis=1) + jnp.sum(w_up.astype(F32) * grad_up, axis=1)
    ) / mlp_gain.astype(F32)
    return (
        output[None],
        input_grad[None],
        grad_attn_gain,
        grad_query,
        grad_key,
        grad_value,
        grad_output_proj,
        grad_mlp_gain,
        grad_gate,
        grad_up,
        grad_down,
    )


def solution(mesh):
    shape = (mesh.shape["dp"] // 2, 2, mesh.shape["sp"])
    cores = Mesh(mesh.devices.reshape(shape), EVERY)
    token_spec = P(MEMBERS, "sp", None)
    vector_spec = P(EVERY)
    weight_spec = P(EVERY, None)
    return jax.shard_map(
        local,
        mesh=cores,
        in_specs=(
            token_spec,
            token_spec,
            P(MEMBERS, None),
            vector_spec,
            weight_spec,
            weight_spec,
            weight_spec,
            weight_spec,
            vector_spec,
            weight_spec,
            weight_spec,
            weight_spec,
        ),
        out_specs=(
            token_spec,
            token_spec,
            vector_spec,
            weight_spec,
            weight_spec,
            weight_spec,
            weight_spec,
            vector_spec,
            weight_spec,
            weight_spec,
            weight_spec,
        ),
        check_vma=False,
    )
```

```python
import math

import jax
import jax.numpy as jnp
from jax import lax
from jax.experimental import pallas as pl
from jax.experimental.pallas import tpu as pltpu
from jax.sharding import Mesh, PartitionSpec as P

HQ = 32
KEY_VALUE_HEADS = 4
HEAD_SIZE = 64
UNIT = 128
DOC_UNITS = 8
LANES = 128
GROUP = HQ // KEY_VALUE_HEADS
QUERY_WIDTH = HQ * HEAD_SIZE
KEY_WIDTH = KEY_VALUE_HEADS * HEAD_SIZE
PROJECT = QUERY_WIDTH + 2 * KEY_WIDTH
BLOCK = GROUP * HEAD_SIZE

EPSILON = 1e-05
MASKED = -1e30
SCALE = HEAD_SIZE ** (-0.5)
F32 = jnp.float32
BF16 = jnp.bfloat16
MEMBERS = ("chip", "core")
EVERY = ("chip", "core", "sp")
VMEM_LIMIT = 48 * 1024 * 1024
NO_COST = pl.CostEstimate(flops=0, bytes_accessed=0, transcendentals=0)


def cost(flops):
    return pl.CostEstimate(flops=int(flops), bytes_accessed=0, transcendentals=0)


def doc_layout(unit_lengths, places):
    token_lengths = unit_lengths * UNIT
    ends = jnp.cumsum(token_lengths)
    passed = places[:, None] >= ends[None, :]
    return jnp.sum(jnp.where(passed, token_lengths[None, :], 0), axis=1)


def rope_tables(positions):
    half_dim = HEAD_SIZE // 2
    inverse = jnp.power(10000.0, jnp.arange(half_dim, dtype=F32) * (-2.0 / HEAD_SIZE))
    angles = positions.astype(F32)[:, None] * inverse[None, :]
    return jnp.tile(jnp.cos(angles), (1, 4)), jnp.tile(jnp.sin(angles), (1, 4))


def key_pieces(length, shard, docs):
    units, per = length // UNIT, shard // UNIT
    longest = min(DOC_UNITS, units - 2)
    needed = 1
    for unit in range(units):
        earliest = max(0, unit - longest + 1)
        if docs == 2 and unit >= longest:
            earliest = max(earliest, units - longest)
        needed = max(needed, unit // per - earliest // per + 1)
    return needed


def contract_last(left, right):
    return lax.dot_general(left, right, (((1,), (1,)), ((), ())), preferred_element_type=F32)


def contract_rows(left, right):
    return lax.dot_general(left, right, (((0,), (0,)), ((), ())), preferred_element_type=F32)


def first_half(shape):
    lane = lax.broadcasted_iota(jnp.int32, shape, 1)
    return lane % HEAD_SIZE < HEAD_SIZE // 2


def half_swap(values):
    half_dim, lanes = HEAD_SIZE // 2, values.shape[1]
    return jnp.where(
        first_half(values.shape),
        pltpu.roll(values, lanes - half_dim, 1),
        pltpu.roll(values, half_dim, 1),
    )


def member_product(by_rows, chips, values, own, other, core, extras, out_shapes, finish, name):
    tokens = values.shape[0]
    block, columns = own.shape[0] // chips, own.shape[1]
    width = columns if by_rows else 2 * own.shape[0]

    def kernel(core_ref, values_ref, own_ref, other_ref, *refs):
        extra_refs, out_refs, total_ref = refs[: len(extras)], refs[len(extras) : -1], refs[-1]
        chip, mine = pl.program_id(0), core_ref[0]
        places = [
            pl.ds(pl.multiple_of((chip * 2 + c) * block, LANES), block) for c in (mine, 1 - mine)
        ]
        if by_rows:
            part = jnp.dot(values_ref[:, places[0]], own_ref[...], preferred_element_type=F32)
            part = part + jnp.dot(values_ref[:, places[1]], other_ref[...], preferred_element_type=F32)

            @pl.when(chip == 0)
            def _():
                total_ref[...] = part

            @pl.when(chip > 0)
            def _():
                total_ref[...] += part
        else:
            used = values_ref.shape[1]
            total_ref[:, places[0]] = contract_last(values_ref[...], own_ref[:, :used])
            total_ref[:, places[1]] = contract_last(values_ref[...], other_ref[:, :used])

        @pl.when(chip == chips - 1)
        def _():
            finish(total_ref, extra_refs, out_refs)

    def whole(shape):
        return pl.BlockSpec(shape, lambda i: (0,) * len(shape))

    return pl.pallas_call(
        kernel,
        grid=(chips,),
        in_specs=[
            pl.BlockSpec(memory_space=pltpu.SMEM),
            whole(values.shape),
            pl.BlockSpec((block, columns), lambda i: (i, 0)),
            pl.BlockSpec((block, columns), lambda i: (i, 0)),
        ]
        + [whole(e.shape) for e in extras],
        out_specs=[whole(o.shape) for o in out_shapes],
        out_shape=out_shapes,
        scratch_shapes=[pltpu.VMEM((tokens, width), F32)],
        compiler_params=pltpu.CompilerParams(vmem_limit_bytes=VMEM_LIMIT),
        cost_estimate=NO_COST,
        name=name,
    )(core, values, own, other, *extras)


def project_kernel(
    core_ref, scaled_ref, own_ref, other_ref, cos_ref, sin_ref, out_ref, normed_ref, gains_ref, total_ref
):
    chip, mine = pl.program_id(0), core_ref[0]
    block = own_ref.shape[0]
    part = None
    for ref, c in ((own_ref, mine), (other_ref, 1 - mine)):
        place = pl.ds(pl.multiple_of((chip * 2 + c) * block, LANES), block)
        gains = ref[:, PROJECT : PROJECT + LANES].astype(F32).T[:8]
        gains_ref[:, place] = gains
        normed = (scaled_ref[:, place] * gains[:1]).astype(BF16)
        normed_ref[:, place] = normed
        term = jnp.dot(normed, ref[:, :PROJECT], preferred_element_type=F32)
        part = term if part is None else part + term

    @pl.when(chip == 0)
    def _():
        total_ref[...] = part

    @pl.when(chip > 0)
    def _():
        total_ref[...] += part

    @pl.when(chip == pl.num_programs(0) - 1)
    def _():
        cosine = jnp.concatenate([cos_ref[...]] * (BLOCK // LANES), axis=1)
        sine = jnp.concatenate([sin_ref[...]] * (BLOCK // LANES), axis=1)
        for step in range(PROJECT // BLOCK):
            where = slice(step * BLOCK, (step + 1) * BLOCK)
            values = total_ref[:, where]
            swapped = half_swap(values)
            turned = values * cosine + jnp.where(first_half(values.shape), -swapped, swapped) * sine
            if step < QUERY_WIDTH // BLOCK:
                result = turned * SCALE
            else:
                lane = lax.broadcasted_iota(jnp.int32, values.shape, 1)
                result = jnp.where(lane % LANES < HEAD_SIZE, turned, values)
            out_ref[:, where] = result.astype(BF16)


def projections(chips, scaled, own, other, core, cosine, sine):
    tokens, width = scaled.shape
    block, columns = own.shape[0] // chips, own.shape[1]

    def whole(shape):
        return pl.BlockSpec(shape, lambda i: (0, 0))

    return pl.pallas_call(
        project_kernel,
        grid=(chips,),
        in_specs=[
            pl.BlockSpec(memory_space=pltpu.SMEM),
            whole((tokens, width)),
            pl.BlockSpec((block, columns), lambda i: (i, 0)),
            pl.BlockSpec((block, columns), lambda i: (i, 0)),
            whole((tokens, LANES)),
            whole((tokens, LANES)),
        ],
        out_specs=[whole((tokens, PROJECT)), whole((tokens, width)), whole((8, width))],
        out_shape=[
            jax.ShapeDtypeStruct((tokens, PROJECT), BF16),
            jax.ShapeDtypeStruct((tokens, width), BF16),
            jax.ShapeDtypeStruct((8, width), F32),
        ],
        scratch_shapes=[pltpu.VMEM((tokens, PROJECT), F32)],
        compiler_params=pltpu.CompilerParams(vmem_limit_bytes=VMEM_LIMIT),
        cost_estimate=NO_COST,
        name="project",
    )(core, scaled, own, other, cosine, sine)


def finish_residual(total_ref, extras, outs):
    tokens_ref, gain_ref = extras
    resid = tokens_ref[...].astype(F32) + total_ref[...]
    inverse = lax.rsqrt(jnp.mean(resid * resid, axis=1, keepdims=True) + EPSILON)
    outs[0][...] = resid
    outs[1][...] = (resid * inverse * gain_ref[...]).astype(BF16)


def finish_cast(total_ref, extras, outs):
    outs[0][...] = total_ref[...].astype(BF16)


def finish_input_grad(total_ref, extras, outs):
    d_resid_ref, tokens_ref, gain_ref = extras
    tokens = tokens_ref[...].astype(F32)
    inverse = lax.rsqrt(jnp.mean(tokens * tokens, axis=1, keepdims=True) + EPSILON)
    mixed = total_ref[...] * gain_ref[...]
    along = jnp.mean(mixed * tokens, axis=1, keepdims=True)
    grad = d_resid_ref[...] + inverse * mixed - tokens * (inverse * inverse * inverse) * along
    outs[0][...] = grad.astype(BF16)


def attend_kernel(query_ref, pair_ref, bias_ref, out_ref, log_ref):
    key, value = pair_ref[:, :HEAD_SIZE], pair_ref[:, HEAD_SIZE:]
    for two in range(GROUP // 2):
        parts = []
        for head in (2 * two, 2 * two + 1):
            query = query_ref[:, head * HEAD_SIZE : (head + 1) * HEAD_SIZE]
            scores = contract_last(key, query) + bias_ref[...]
            largest = jnp.max(scores, axis=0, keepdims=True)
            weights = jnp.exp(scores - largest)
            totals = jnp.sum(weights, axis=0, keepdims=True)
            parts.append(contract_rows(value, weights.astype(BF16)) / totals)
            log_ref[head : head + 1, :] = largest + jnp.log(totals)
        both = jnp.concatenate(parts, axis=0)
        out_ref[:, two * LANES : (two + 1) * LANES] = both.T.astype(BF16)


def attend(project, pairs, bias):
    tokens, keys = project.shape[0], pairs.shape[0]
    return pl.pallas_call(
        attend_kernel,
        grid=(KEY_VALUE_HEADS,),
        in_specs=[
            pl.BlockSpec((tokens, BLOCK), lambda i: (0, i)),
            pl.BlockSpec((keys, LANES), lambda i: (0, i)),
            pl.BlockSpec((keys, tokens), lambda i: (0, 0)),
        ],
        out_specs=[
            pl.BlockSpec((tokens, BLOCK), lambda i: (0, i)),
            pl.BlockSpec((GROUP, tokens), lambda i: (i, 0)),
        ],
        out_shape=[
            jax.ShapeDtypeStruct((tokens, QUERY_WIDTH), BF16),
            jax.ShapeDtypeStruct((HQ, tokens), F32),
        ],
        compiler_params=pltpu.CompilerParams(vmem_limit_bytes=VMEM_LIMIT),
        cost_estimate=NO_COST,
        name="attend",
    )(project, pairs, bias)


def attend_back_kernel(
    query_ref, grad_ref, pair_ref, log_ref, bias_ref, cos_ref, sin_ref, d_query_ref, *d_pair_refs
):
    key, value = pair_ref[:, :HEAD_SIZE], pair_ref[:, HEAD_SIZE:]
    d_key = jnp.zeros((key.shape[0], HEAD_SIZE), F32)
    d_value = jnp.zeros((key.shape[0], HEAD_SIZE), F32)
    for two in range(GROUP // 2):
        parts = []
        for head in (2 * two, 2 * two + 1):
            query = query_ref[:, head * HEAD_SIZE : (head + 1) * HEAD_SIZE]
            grad = grad_ref[:, head * HEAD_SIZE : (head + 1) * HEAD_SIZE]
            scores = contract_last(key, query) + bias_ref[...]
            probs = jnp.exp(scores - log_ref[head : head + 1, :])
            d_probs = contract_last(value, grad)
            row_dot = jnp.sum(probs * d_probs, axis=0, keepdims=True)
            d_scores = (probs * (d_probs - row_dot)).astype(BF16)
            d_value = d_value + jnp.dot(probs.astype(BF16), grad, preferred_element_type=F32)
            d_key = d_key + jnp.dot(d_scores, query, preferred_element_type=F32)
            parts.append(contract_rows(key, d_scores) * SCALE)
        both = jnp.concatenate(parts, axis=0).T.astype(BF16).astype(F32)
        swapped = half_swap(both * sin_ref[...])
        back = both * cos_ref[...] + jnp.where(first_half(both.shape), swapped, -swapped)
        d_query_ref[:, two * LANES : (two + 1) * LANES] = back.astype(BF16)
    d_pair = jnp.concatenate([d_key, d_value], axis=1)
    shard = query_ref.shape[0]
    for piece, ref in enumerate(d_pair_refs):
        ref[...] = d_pair[piece * shard : (piece + 1) * shard].astype(ref.dtype)


def attend_back(project, grads, pairs, logs, bias, cosine, sine):
    tokens, keys = project.shape[0], pairs.shape[0]
    return pl.pallas_call(
        attend_back_kernel,
        grid=(KEY_VALUE_HEADS,),
        in_specs=[
            pl.BlockSpec((tokens, BLOCK), lambda i: (0, i)),
            pl.BlockSpec((tokens, BLOCK), lambda i: (0, i)),
            pl.BlockSpec((keys, LANES), lambda i: (0, i)),
            pl.BlockSpec((GROUP, tokens), lambda i: (i, 0)),
            pl.BlockSpec((keys, tokens), lambda i: (0, 0)),
            pl.BlockSpec((tokens, LANES), lambda i: (0, 0)),
            pl.BlockSpec((tokens, LANES), lambda i: (0, 0)),
        ],
        out_specs=[
            pl.BlockSpec((tokens, BLOCK), lambda i: (0, i)),
        ]
        + [pl.BlockSpec((tokens, LANES), lambda i: (0, i))] * (keys // tokens),
        out_shape=[
            jax.ShapeDtypeStruct((tokens, QUERY_WIDTH), BF16),
            jax.ShapeDtypeStruct((tokens, 2 * KEY_WIDTH), F32),
        ]
        + [jax.ShapeDtypeStruct((tokens, 2 * KEY_WIDTH), BF16)] * (keys // tokens - 1),
        compiler_params=pltpu.CompilerParams(vmem_limit_bytes=VMEM_LIMIT),
        cost_estimate=cost(256 * HQ * tokens * keys * HEAD_SIZE),
        name="attend_back",
    )(project, grads, pairs, logs, bias, cosine, sine)


def load_rows(sources, held, sems):
    copies = []
    for (ref, first), to in zip(sources, held):
        for j in range(ref.shape[0]):
            part = ref.at[j, :, :, pl.ds(first, to.shape[3])]
            copies.append(pltpu.make_async_copy(part, to.at[:, j], sems.at[len(copies)]))
            copies[-1].start()
    for copy in copies:
        copy.wait()


def as_rows(ref):
    return ref[...].reshape(-1, ref.shape[3])


def feed_forward(normed, grads, weight, local):
    tokens, width = normed.shape
    sp_count, dp_count, rows, columns = weight.shape
    block = min(tokens, 256)
    both, last = lanes_of(2 * local), lanes_of(local)

    def kernel(normed_ref, grad_ref, weight_ref, hidden_ref, d_both_ref, held, sems):
        @pl.when(pl.program_id(0) == 0)
        def _():
            load_rows([(weight_ref, 0)], [held], sems)

        weights = held[...].reshape(width, columns)
        pair = jnp.dot(normed_ref[...], weights[:, :both], preferred_element_type=F32)
        d_hidden = jnp.dot(grad_ref[...], weights[:, both:], preferred_element_type=F32)
        gate, up = pair[:, :last], moved(pair, -local)[:, :last]
        sigmoid_gate = jax.nn.sigmoid(gate)
        activated = gate * sigmoid_gate
        hidden_ref[...] = first_lanes(activated * up, local).astype(BF16)
        d_gate = first_lanes(d_hidden * up * (sigmoid_gate * (1.0 + gate * (1.0 - sigmoid_gate))), local)
        d_up = first_lanes(d_hidden * activated, local)
        d_both_ref[...] = (widened(d_gate, both) + moved(widened(d_up, both), local)).astype(BF16)

    return pl.pallas_call(
        kernel,
        grid=(tokens // block,),
        in_specs=[
            pl.BlockSpec((block, width), lambda i: (i, 0)),
            pl.BlockSpec((block, width), lambda i: (i, 0)),
            pl.BlockSpec(memory_space=pl.ANY),
        ],
        out_specs=[
            pl.BlockSpec((block, last), lambda i: (i, 0)),
            pl.BlockSpec((block, both), lambda i: (i, 0)),
        ],
        out_shape=[
            jax.ShapeDtypeStruct((tokens, last), BF16),
            jax.ShapeDtypeStruct((tokens, both), BF16),
        ],
        scratch_shapes=[
            pltpu.VMEM((dp_count, sp_count, rows, columns), BF16),
            pltpu.SemaphoreType.DMA((sp_count,)),
        ],
        compiler_params=pltpu.CompilerParams(vmem_limit_bytes=VMEM_LIMIT),
        cost_estimate=NO_COST,
        name="feed_forward",
    )(normed, grads, weight)


def times_weights(values, weights):
    terms = len(values)
    count, columns = values[0].shape
    sp_count, dp_count, rows, _ = weights[0][0].shape
    width = sp_count * dp_count * rows
    block = min(count, 256)

    def kernel(*refs):
        value_refs, weight_refs = refs[:terms], refs[terms : 2 * terms]
        out_ref, held, sems = refs[2 * terms], refs[2 * terms + 1 : -1], refs[-1]

        @pl.when(pl.program_id(0) == 0)
        def _():
            load_rows([(r, w[1]) for r, w in zip(weight_refs, weights)], held, sems)

        total = contract_last(value_refs[0][...], as_rows(held[0]))
        for ref, weight in zip(value_refs[1:], held[1:]):
            total = total + contract_last(ref[...], as_rows(weight))
        out_ref[...] = total.astype(BF16)

    return pl.pallas_call(
        kernel,
        grid=(count // block,),
        in_specs=[pl.BlockSpec((block, columns), lambda i: (i, 0))] * terms
        + [pl.BlockSpec(memory_space=pl.ANY)] * terms,
        out_specs=pl.BlockSpec((block, width), lambda i: (i, 0)),
        out_shape=jax.ShapeDtypeStruct((count, width), BF16),
        scratch_shapes=[pltpu.VMEM((dp_count, sp_count, rows, columns), BF16)] * terms
        + [pltpu.SemaphoreType.DMA((terms * sp_count,))],
        compiler_params=pltpu.CompilerParams(vmem_limit_bytes=VMEM_LIMIT),
        cost_estimate=NO_COST,
        name="times_weights",
    )(*values, *(w[0] for w in weights))


def row_grad(dealt, rights, core, chips):
    tokens, columns = rights[0].shape
    rows = dealt.shape[1]
    block = min(columns, 512)

    def kernel(core_ref, left_ref, left2_ref, right_ref, right2_ref, out_ref):
        total = contract_rows(left_ref[...].reshape(tokens, rows), right_ref[...])
        total = total + contract_rows(left2_ref[...].reshape(tokens, rows), right2_ref[...])
        out_ref[...] = total.astype(BF16)

    dealt = dealt.reshape(chips, 2, tokens // chips, rows)
    part = (chips, 1, tokens // chips, rows)
    return pl.pallas_call(
        kernel,
        grid_spec=pltpu.PrefetchScalarGridSpec(
            num_scalar_prefetch=1,
            grid=(columns // block,),
            in_specs=[
                pl.BlockSpec(part, lambda i, c: (0, c[0], 0, 0)),
                pl.BlockSpec(part, lambda i, c: (0, 1 - c[0], 0, 0)),
                pl.BlockSpec((tokens, block), lambda i, c: (0, i)),
                pl.BlockSpec((tokens, block), lambda i, c: (0, i)),
            ],
            out_specs=pl.BlockSpec((rows, block), lambda i, c: (0, i)),
        ),
        out_shape=jax.ShapeDtypeStruct((rows, columns), BF16),
        compiler_params=pltpu.CompilerParams(vmem_limit_bytes=VMEM_LIMIT),
        cost_estimate=NO_COST,
        name="row_grad",
    )(core, dealt, dealt, *rights)


def dealt_grad(lefts, dealt, width, sp_count, dp_count, core):
    tokens = lefts[0].shape[0]
    columns = dealt.shape[1]
    block = width // dp_count
    rows = block // sp_count
    chips = dp_count // 2

    def kernel(core_ref, left_ref, left2_ref, right_ref, right2_ref, out_ref, done_ref):
        total = contract_rows(left_ref[...], right_ref[...].reshape(tokens, columns))
        total = total + contract_rows(left2_ref[...], right2_ref[...].reshape(tokens, columns))
        out_ref[...] = total.astype(BF16).reshape(sp_count, 1, rows, columns)
        done_ref[...] = jnp.zeros_like(done_ref)

    dealt = dealt.reshape(chips, 2, tokens // chips, columns)
    part = (chips, 1, tokens // chips, columns)
    total, done = pl.pallas_call(
        kernel,
        grid_spec=pltpu.PrefetchScalarGridSpec(
            num_scalar_prefetch=1,
            grid=(dp_count,),
            in_specs=[
                pl.BlockSpec((tokens, block), lambda i, c: (0, i)),
                pl.BlockSpec((tokens, block), lambda i, c: (0, i)),
                pl.BlockSpec(part, lambda i, c: (0, c[0], 0, 0)),
                pl.BlockSpec(part, lambda i, c: (0, 1 - c[0], 0, 0)),
            ],
            out_specs=[
                pl.BlockSpec((sp_count, 1, rows, columns), lambda i, c: (0, i, 0, 0)),
                pl.BlockSpec((8, LANES), lambda i, c: (0, 0)),
            ],
        ),
        out_shape=[
            jax.ShapeDtypeStruct((sp_count, dp_count, rows, columns), BF16),
            jax.ShapeDtypeStruct((8, LANES), F32),
        ],
        compiler_params=pltpu.CompilerParams(vmem_limit_bytes=VMEM_LIMIT),
        cost_estimate=NO_COST,
        name="dealt_grad",
    )(core, *lefts, dealt, dealt)
    return total.reshape(width, columns), done


def weight_grad(lefts, rights, width, sp_count, dp_count):
    tokens = lefts[0].shape[0]
    columns = rights[0].shape[1]
    block = width // dp_count
    rows = block // sp_count

    def kernel(left_ref, left2_ref, right_ref, right2_ref, out_ref, done_ref):
        total = contract_rows(left_ref[...], right_ref[...])
        total = total + contract_rows(left2_ref[...], right2_ref[...])
        out_ref[...] = total.astype(BF16).reshape(sp_count, 1, rows, columns)
        done_ref[...] = jnp.zeros_like(done_ref)

    total, done = pl.pallas_call(
        kernel,
        grid=(dp_count,),
        in_specs=[pl.BlockSpec((tokens, block), lambda i: (0, i))] * 2
        + [pl.BlockSpec((tokens, columns), lambda i: (0, 0))] * 2,
        out_specs=[
            pl.BlockSpec((sp_count, 1, rows, columns), lambda i: (0, i, 0, 0)),
            pl.BlockSpec((8, LANES), lambda i: (0, 0)),
        ],
        out_shape=[
            jax.ShapeDtypeStruct((sp_count, dp_count, rows, columns), BF16),
            jax.ShapeDtypeStruct((8, LANES), F32),
        ],
        compiler_params=pltpu.CompilerParams(vmem_limit_bytes=VMEM_LIMIT),
        cost_estimate=NO_COST,
        name="weight_grad",
    )(*lefts, *rights)
    return total.reshape(width, columns), done


def assemble(pieces, starts, first=0, columns=None, deps=()):
    count = len(pieces)
    total = sum(piece.shape[0] for piece in pieces)
    columns = columns or pieces[0].shape[1]

    def kernel(starts_ref, *refs):
        out_ref, held, in_sems, out_sems = refs[count + len(deps) :]
        inward, outward = [], []
        for i in range(count):
            place = pl.ds(pl.multiple_of(starts_ref[i], 32), pieces[i].shape[0])
            piece = refs[i].at[:, pl.ds(first, columns)]
            inward.append(pltpu.make_async_copy(piece, held.at[place, :], in_sems.at[i]))
            outward.append(
                pltpu.make_async_copy(held.at[place, :], out_ref.at[place, :], out_sems.at[i])
            )
            inward[-1].start()
        for i in range(count):
            inward[i].wait()
            outward[i].start()
        for copy in outward:
            copy.wait()

    return pl.pallas_call(
        kernel,
        in_specs=[pl.BlockSpec(memory_space=pltpu.SMEM)]
        + [pl.BlockSpec(memory_space=pl.ANY)] * (count + len(deps)),
        out_specs=pl.BlockSpec(memory_space=pl.ANY),
        out_shape=jax.ShapeDtypeStruct((total, columns), pieces[0].dtype),
        scratch_shapes=[
            pltpu.VMEM((total, columns), pieces[0].dtype),
            pltpu.SemaphoreType.DMA((count,)),
            pltpu.SemaphoreType.DMA((count,)),
        ],
        compiler_params=pltpu.CompilerParams(vmem_limit_bytes=VMEM_LIMIT),
        cost_estimate=NO_COST,
        name="assemble",
    )(jnp.stack([jnp.asarray(s, jnp.int32) for s in starts]), *pieces, *deps)


def windows(arrays, starts, sizes, deps=()):
    count, rows, total = len(starts), arrays[0].shape[0], sum(sizes)

    def kernel(*refs):
        out_ref = refs[-1]
        for k in range(count):
            at = 0
            for i, size in enumerate(sizes):
                out_ref[k * rows : (k + 1) * rows, at : at + size] = refs[i][:, starts[k][i] : starts[k][i] + size]
                at += size

    return pl.pallas_call(
        kernel,
        in_specs=[pl.BlockSpec(memory_space=pltpu.VMEM)] * len(arrays)
        + [pl.BlockSpec(memory_space=pl.ANY)] * len(deps),
        out_specs=pl.BlockSpec(memory_space=pltpu.VMEM),
        out_shape=jax.ShapeDtypeStruct((count * rows, total), arrays[0].dtype),
        compiler_params=pltpu.CompilerParams(vmem_limit_bytes=VMEM_LIMIT),
        cost_estimate=NO_COST,
        name="windows",
    )(*arrays, *deps)


def summed(left, right):
    rows, columns = left.shape
    block = min(rows, 256)

    def kernel(left_ref, right_ref, out_ref):
        out_ref[...] = (left_ref[...].astype(F32) + right_ref[...].astype(F32)).astype(BF16)

    spec = pl.BlockSpec((block, columns), lambda i: (i, 0))
    return pl.pallas_call(
        kernel,
        grid=(rows // block,),
        in_specs=[spec] * 2,
        out_specs=spec,
        out_shape=jax.ShapeDtypeStruct(left.shape, BF16),
        cost_estimate=NO_COST,
        compiler_params=pltpu.CompilerParams(vmem_limit_bytes=VMEM_LIMIT),
        name="summed",
    )(left, right)


def residual_grad(arrived, grads, resid, gain):
    chips, tokens, width = arrived.shape
    block = min(tokens, 64)

    def kernel(arrived_ref, grad_ref, resid_ref, gain_ref, d_resid_ref, rounded_ref):
        total = arrived_ref[0].astype(F32)
        for i in range(1, chips):
            total = total + arrived_ref[i].astype(F32)
        resid = resid_ref[...]
        inverse = lax.rsqrt(jnp.mean(resid * resid, axis=1, keepdims=True) + EPSILON)
        mixed = total * gain_ref[...]
        along = jnp.mean(mixed * resid, axis=1, keepdims=True)
        d_resid = grad_ref[...].astype(F32) + inverse * mixed - resid * (inverse * inverse * inverse) * along
        d_resid_ref[...] = d_resid
        rounded_ref[...] = d_resid.astype(BF16)

    spec = pl.BlockSpec((block, width), lambda i: (i, 0))
    return pl.pallas_call(
        kernel,
        grid=(tokens // block,),
        in_specs=[
            pl.BlockSpec((chips, block, width), lambda i: (0, i, 0)),
            spec,
            spec,
            pl.BlockSpec((1, width), lambda i: (0, 0)),
        ],
        out_specs=[spec, spec],
        out_shape=[jax.ShapeDtypeStruct((tokens, width), F32), jax.ShapeDtypeStruct((tokens, width), BF16)],
        compiler_params=pltpu.CompilerParams(vmem_limit_bytes=VMEM_LIMIT),
        cost_estimate=NO_COST,
        name="residual_grad",
    )(arrived, grads, resid, gain)


def pair_back(own, arrived, cosine, sine):
    tokens, columns = own.shape
    count = len(arrived)

    def kernel(own_ref, cos_ref, sin_ref, *refs):
        total = own_ref[...]
        for ref in refs[:count]:
            total = total + ref[...].astype(F32)
        total = total.astype(BF16).astype(F32)
        times = columns // LANES
        cosine = jnp.concatenate([cos_ref[...]] * times, axis=1)
        sine = jnp.concatenate([sin_ref[...]] * times, axis=1)
        swapped = half_swap(total * sine)
        back = total * cosine + jnp.where(first_half(total.shape), swapped, -swapped)
        lane = lax.broadcasted_iota(jnp.int32, total.shape, 1)
        refs[count][...] = jnp.where(lane % LANES < HEAD_SIZE, back, total).astype(BF16)

    return pl.pallas_call(
        kernel,
        out_shape=jax.ShapeDtypeStruct((tokens, columns), BF16),
        compiler_params=pltpu.CompilerParams(vmem_limit_bytes=VMEM_LIMIT),
        cost_estimate=NO_COST,
        name="pair_back",
    )(own, cosine, sine, *arrived)


def lanes_of(count):
    return -(-count // LANES) * LANES


def moved(values, by):
    return values if by % values.shape[1] == 0 else pltpu.roll(values, by % values.shape[1], 1)


def first_lanes(values, count):
    lane = lax.broadcasted_iota(jnp.int32, values.shape, 1)
    return jnp.where(lane < count, values, 0.0)


def widened(values, lanes):
    if values.shape[1] >= lanes:
        return values[:, :lanes]
    return jnp.concatenate([values, jnp.zeros((values.shape[0], lanes - values.shape[1]), values.dtype)], axis=1)


def pack_columns(gate, up, down, dp_count):
    rows, ff = gate.shape
    local = ff // dp_count
    together = LANES // math.gcd(local, LANES)
    group = together * local
    both, last = lanes_of(2 * local), lanes_of(local)

    def kernel(gate_ref, up_ref, down_ref, out_ref):
        for m in range(dp_count):
            place = slice(m // together * group, m // together * group + group)
            parts = [
                first_lanes(moved(ref[:, place].astype(F32), -(m % together) * local), local)
                for ref in (gate_ref, up_ref, down_ref)
            ]
            pair = widened(parts[0], both) + moved(widened(parts[1], both), local)
            out_ref[m * rows : (m + 1) * rows, :both] = pair.astype(BF16)
            out_ref[m * rows : (m + 1) * rows, both:] = widened(parts[2], last).astype(BF16)

    return pl.pallas_call(
        kernel,
        out_shape=jax.ShapeDtypeStruct((dp_count * rows, both + last), BF16),
        compiler_params=pltpu.CompilerParams(vmem_limit_bytes=VMEM_LIMIT),
        cost_estimate=NO_COST,
        name="pack_columns",
    )(gate, up, down)


def unpack_columns(packed, ff):
    dp_count, rows, _ = packed.shape
    local = ff // dp_count
    together = LANES // math.gcd(local, LANES)
    group = together * local
    both = lanes_of(2 * local)

    def kernel(packed_ref, *outs):
        for first in range(0, dp_count, together):
            sums = [jnp.zeros((rows, group), F32) for _ in outs]
            for i in range(together):
                block = packed_ref[first + i].astype(F32)
                pair, last = block[:, :both], block[:, both:]
                for k, part in enumerate((pair, moved(pair, -local), last)):
                    sums[k] = sums[k] + moved(widened(first_lanes(part, local), group), i * local)
            place = slice(first * local, first * local + group)
            for out, total in zip(outs, sums):
                out[:, place] = total

    return pl.pallas_call(
        kernel,
        out_shape=[jax.ShapeDtypeStruct((rows, ff), F32)] * 3,
        compiler_params=pltpu.CompilerParams(vmem_limit_bytes=VMEM_LIMIT),
        cost_estimate=NO_COST,
        name="unpack_columns",
    )(packed)


def after(value, *others):
    def kernel(*refs):
        del refs

    return pl.pallas_call(
        kernel,
        in_specs=[pl.BlockSpec(memory_space=pl.ANY)] * (1 + len(others)),
        out_specs=pl.BlockSpec(memory_space=pl.ANY),
        out_shape=jax.ShapeDtypeStruct(value.shape, value.dtype),
        input_output_aliases={0: 0},
        cost_estimate=NO_COST,
        name="after",
    )(value, *others)


def spread(value, axis, *others):
    count, rows = lax.axis_size(axis), value.shape[0]
    copies = jnp.broadcast_to(value[None], (count,) + value.shape).reshape(count * rows, -1)
    if others:
        copies = after(copies, *others)
    return lax.all_to_all(copies, axis, split_axis=0, concat_axis=0, tiled=True)


def sp_rows(value, sp_count, sp_index):
    rows = value.shape[0]
    pieces, starts = [value], [sp_index * rows]
    for j in range(1, sp_count):
        pieces.append(lax.ppermute(value, "sp", [(i, (i + j) % sp_count) for i in range(sp_count)]))
        starts.append((sp_index - j) % sp_count * rows)
    return assemble(pieces, starts)


def swap_cores(value):
    return lax.ppermute(value, "core", [(0, 1), (1, 0)])


def deal(value, axis):
    return lax.all_to_all(value, axis, split_axis=0, concat_axis=0, tiled=True)


def shift(value, count, by):
    pairs = [(i, i + by) for i in range(count) if 0 <= i + by < count]
    return lax.ppermute(value, "sp", pairs)


def local(
    inputs,
    cotangent,
    unit_lengths,
    attn_gain,
    w_query,
    key_weight,
    value_weight,
    w_output,
    mlp_gain,
    w_gate,
    w_up,
    w_down,
):
    chips = lax.axis_size("chip")
    dp_count = 2 * chips
    sp_count = lax.axis_size("sp")
    core = lax.axis_index("core")
    member = lax.axis_index("chip") * 2 + core
    core_only = core.astype(jnp.int32)[None]
    sp_index = lax.axis_index("sp")
    shard = inputs.shape[1]
    width = inputs.shape[2]
    length = shard * sp_count
    rows = w_query.shape[0]
    ff = w_gate.shape[1]
    query_local = QUERY_WIDTH // dp_count
    heads = range(KEY_VALUE_HEADS)
    members = range(dp_count)

    def head_columns(array, head):
        return array[:, head * HEAD_SIZE : (head + 1) * HEAD_SIZE]

    ff_local = ff // dp_count
    both_lanes = lanes_of(2 * ff_local)

    pair_columns = [head_columns(w, h) for h in heads for w in (key_weight, value_weight)]
    gains_local = jnp.pad(jnp.stack([attn_gain, mlp_gain], axis=1), ((0, 0), (0, LANES - 2)))
    in_local = jnp.concatenate([w_query] + pair_columns + [gains_local], axis=1)
    in_group = sp_rows(in_local, sp_count, sp_index)
    ff_mine = deal(pack_columns(w_gate, w_up, w_down, dp_count), MEMBERS)

    def along_sp(mine):
        return lax.all_gather(mine, "sp", axis=0).reshape(sp_count, dp_count, rows, mine.shape[1])

    out_group = sp_rows(w_output, sp_count, sp_index)
    ff_weight = along_sp(after(ff_mine, in_group))
    pair_weight, down_weight = (ff_weight, 0), (ff_weight, both_lanes)
    in_own = after(spread(in_group, "chip", ff_mine), out_group)
    in_other = swap_cores(in_own)
    out_own = spread(out_group, "chip", in_own)
    places = sp_index * shard + jnp.arange(shard, dtype=jnp.int32)
    begins = doc_layout(unit_lengths[0], places)
    cosine, sine = rope_tables(places - begins)
    pieces = key_pieces(length, shard, unit_lengths.shape[1])
    key_places = jnp.concatenate([places - j * shard for j in range(pieces)])[:, None]
    bias = jnp.where((key_places <= places[None]) & (key_places >= begins[None]), 0.0, MASKED)
    tokens_in = inputs[0].astype(F32)
    inv_one = lax.rsqrt(jnp.mean(tokens_in * tokens_in, axis=1, keepdims=True) + EPSILON)
    project, normed_one, gains = projections(
        chips, tokens_in * inv_one, in_own, in_other, core_only, cosine, sine
    )
    gain_one, gain_two = gains[:1], gains[1:2]
    pair = project[:, QUERY_WIDTH:]
    pairs = jnp.concatenate([pair] + [shift(pair, sp_count, j) for j in range(1, pieces)], axis=0)
    out_own = after(out_own, pairs)
    out_other = swap_cores(out_own)
    grad_own = spread(cotangent[0], "chip", out_own)
    grad_other = swap_cores(grad_own)
    attended, logs = attend(project, after(pairs, out_own), bias)
    resid, normed_two = member_product(
        False, chips, attended, out_own, out_other, core_only, [inputs[0], gain_two],
        [jax.ShapeDtypeStruct((shard, width), F32), jax.ShapeDtypeStruct((shard, width), BF16)],
        finish_residual, "out_project",
    )

    two_own = spread(normed_two, "chip", grad_own, ff_weight)
    two_other = swap_cores(two_own)
    normed_own = spread(normed_one, "chip", two_own)
    normed_other = swap_cores(normed_own)
    attended_own = spread(attended, "chip", normed_own)
    attended_other = swap_cores(attended_own)
    hidden_own, d_both_own = feed_forward(two_own, grad_own, ff_weight, ff_local)
    hidden_other, d_both_other = feed_forward(two_other, grad_other, ff_weight, ff_local)

    def for_sp(lefts, rights):
        return weight_grad(lefts, rights, width, sp_count, dp_count)

    def over_sp(total):
        return lax.psum_scatter(total, "sp", scatter_dimension=0, tiled=True)

    def chip_sums(own, other):
        return summed(own, swap_cores(other))

    down_total, down_done = for_sp([grad_own, grad_other], [hidden_own, hidden_other])
    summed_down = over_sp(down_total)
    d_both_other = after(d_both_other, down_total, normed_own)
    d_normed_other = times_weights([d_both_other], [pair_weight])
    d_both_own = after(d_both_own, d_normed_other)
    d_normed_own = times_weights([d_both_own], [pair_weight])
    d_normed_sums = after(chip_sums(d_normed_own, d_normed_other), attended_own)
    mlp_other = times_weights([after(hidden_other, d_normed_sums, summed_down)], [down_weight])
    d_both_other = after(d_both_other, mlp_other)
    both_total, both_done = for_sp([two_own, two_other], [d_both_own, d_both_other])
    summed_both = over_sp(after(both_total, summed_down))
    mlp_own = times_weights([after(hidden_own, both_done)], [down_weight])
    mlp_sums = chip_sums(mlp_own, mlp_other)
    d_normed_two = after(deal(d_normed_sums, "chip"), both_done).reshape(chips, shard, width)
    d_resid, d_attn_out = residual_grad(d_normed_two, cotangent[0], resid, gain_two)

    width_local = width // dp_count
    out_rows = deal(windows([d_attn_out], [[m * width_local] for m in members], [width_local]), MEMBERS)
    (d_attended,) = member_product(
        True, chips, d_attn_out, out_own, out_other, core_only, [],
        [jax.ShapeDtypeStruct((shard, QUERY_WIDTH), BF16)], finish_cast, "d_attended",
    )
    def to_owner(summed):
        return deal(summed, MEMBERS).reshape(dp_count, rows, summed.shape[1])

    mlp_arrived = deal(after(mlp_sums, out_rows), "chip")
    d_query, d_pair_own, *d_pairs = attend_back(
        project, after(d_attended, out_rows), pairs, logs, bias, cosine, sine
    )
    pair_arrived = [shift(sent, sp_count, -1 - j) for j, sent in enumerate(d_pairs)]
    out_total = row_grad(after(out_rows, d_query), [attended_own, attended_other], core_only, chips)
    d_pair = pair_back(after(d_pair_own, out_total), pair_arrived, cosine, sine)
    summed_out = over_sp(after(out_total, summed_both, d_pair))
    tile_of = [m * KEY_VALUE_HEADS // dp_count for m in members]
    mlp_out = jnp.sum(mlp_arrived.reshape(chips, shard, width).astype(F32), axis=0)
    output = (resid + mlp_out).astype(BF16)
    project_blocks = windows(
        [d_query, d_pair],
        [[m * query_local, t * LANES] for m, t in zip(members, tile_of)],
        [query_local, LANES],
        [mlp_arrived],
    )
    project_columns = deal(project_blocks, MEMBERS)
    grad_output_proj = summed_out.astype(F32)
    project_total, project_done = dealt_grad(
        [normed_own, normed_other], after(project_columns, summed_out), width, sp_count, dp_count, core_only
    )
    summed_project = over_sp(after(project_total, summed_out))
    d_project = after(jnp.concatenate([d_query, d_pair], axis=1), project_done)
    (input_grad,) = member_product(
        False, chips, d_project, in_own, in_other, core_only, [d_resid, inputs[0], gain_one],
        [jax.ShapeDtypeStruct((shard, width), BF16)], finish_input_grad, "input_grad",
    )
    summed_ff = jnp.concatenate([summed_both, summed_down], axis=1)
    back_ff = to_owner(after(summed_ff, project_done))
    grad_gate, grad_up, grad_down = unpack_columns(after(back_ff, summed_project), ff)
    back = to_owner(after(summed_project, back_ff)).astype(F32)
    grad_query = jnp.concatenate([back[m][:, :query_local] for m in members], axis=1)
    pair_grads = [back[h * dp_count // KEY_VALUE_HEADS][:, query_local:] for h in heads]
    grad_key = jnp.concatenate([g[:, :HEAD_SIZE] for g in pair_grads], axis=1)
    grad_value = jnp.concatenate([g[:, HEAD_SIZE:] for g in pair_grads], axis=1)
    grad_attn_gain = (
        jnp.sum(w_query.astype(F32) * grad_query, axis=1)
        + jnp.sum(key_weight.astype(F32) * grad_key, axis=1)
        + jnp.sum(value_weight.astype(F32) * grad_value, axis=1)
    ) / attn_gain.astype(F32)
    grad_mlp_gain = (
        jnp.sum(w_gate.astype(F32) * grad_gate, axis=1) + jnp.sum(w_up.astype(F32) * grad_up, axis=1)
    ) / mlp_gain.astype(F32)
    return (
        output[None],
        input_grad[None],
        grad_attn_gain,
        grad_query,
        grad_key,
        grad_value,
        grad_output_proj,
        grad_mlp_gain,
        grad_gate,
        grad_up,
        grad_down,
    )


def solution(mesh):
    shape = (mesh.shape["dp"] // 2, 2, mesh.shape["sp"])
    cores = Mesh(mesh.devices.reshape(shape), EVERY)
    token_spec = P(MEMBERS, "sp", None)
    vector_spec = P(EVERY)
    weight_spec = P(EVERY, None)
    return jax.shard_map(
        local,
        mesh=cores,
        in_specs=(
            token_spec,
            token_spec,
            P(MEMBERS, None),
            vector_spec,
            weight_spec,
            weight_spec,
            weight_spec,
            weight_spec,
            vector_spec,
            weight_spec,
            weight_spec,
            weight_spec,
        ),
        out_specs=(
            token_spec,
            token_spec,
            vector_spec,
            weight_spec,
            weight_spec,
            weight_spec,
            weight_spec,
            vector_spec,
            weight_spec,
            weight_spec,
            weight_spec,
        ),
        check_vma=False,
    )
```
